512 devices in a mesh: seq: 64 (over y_lo, z, core), chan: 8 (over y_hi, x).
Axes of the slice: x: 4, y: 4 (y_hi: 2, y_lo: 2; y = y_hi * 2 + y_lo), z: 16, core: 2. Of those that a mesh axis runs over, the one named last changes fastest.
Arguments:
- inputs: float32 [768, 131072], P('chan', 'seq'), may hold values from -6 to 6
- cotangent: float32 [768, 131072], P('chan', 'seq'), may hold values from -6 to 6
- kernel: float32 [768, 256, 512], P('chan', 'seq'), may hold values from -6 to 6
- inner_weight: bfloat16 [256, 256], replicated, may hold values from -0.375 to 0.375
- outer_weight: bfloat16 [512, 512], replicated, may hold values from -0.25 to 0.25
- position_diagonal_scaling: float32 [512, 256], P('seq'), may hold values from -4 to 4
- up_weight: bfloat16 [3072, 96], P('chan'), may hold values from -0.625 to 0.625
- down_weight: bfloat16 [768, 384], P('chan'), may hold values from -0.3125 to 0.3125
Outputs:
- grad_inputs: float32 [768, 131072], P('chan', 'seq')
- grad_kernel: float32 [768, 256, 512], P('chan', 'seq')
- grad_up: float32 [3072, 96], P('chan')
- grad_down: float32 [768, 384], P('chan')
- grad_twiddle: float32 [512, 256], P('seq')
The draws below stay inside these ranges and needn't reach their ends.
All inputs are finite; a program needn't handle non-finite values.
Results may differ from the reference program's by a relative error of at most 0.012.
Values may be sent and summed in bfloat16 or wider, within the bound.
No kernel may reach another device: no remote copies, remote signals or barrier semaphores. Data moves between devices by JAX's collectives and lax.ppermute only.
A program may use at most 64 MiB of HBM per device.

```python
import math
import jax
import jax.numpy as jnp
from jax import lax

D = 768
HID = 3072
NBLK = 8
OUTER = 512
INNER = 256
SEQ = 131072
BW = 96
HB = 384


def level_of(own_key, shape, cuts, low, high):
    gain, own = 1.0, jax.random.fold_in(own_key, 6)
    for dim, blocks in cuts:
        steps = jnp.exp(jax.random.uniform(jax.random.fold_in(own, dim), (blocks,), jnp.float32, low / len(cuts), high / len(cuts)))
        gain = gain * jnp.repeat(steps, shape[dim] // blocks).reshape([-1 if axis == dim else 1 for axis in range(len(shape))])
    return gain


def noise(rng, extent, spread, most, cuts=(), held_as=jnp.bfloat16):
    level = level_of(rng, extent, cuts, -0.22, 0.18) if cuts else 1.0
    entries = jax.random.normal(rng, extent, jnp.float32) * spread * level
    return jnp.minimum(jnp.maximum(entries, -most), most).astype(held_as)


def setup_inputs(seed: int = 0) -> dict:
    splits = jax.random.split(jax.random.key(seed), 9)
    return {
        "inputs": noise(splits[0], (D, SEQ), 1.0, 6.0, ((0, 8), (1, 64)), jnp.float32),
        "cotangent": noise(splits[1], (D, SEQ), 1.0, 6.0, ((0, 8), (1, 64)), jnp.float32),
        "kernel": noise(splits[2], (D, INNER, OUTER), 1.0, 6.0, ((0, 8), (1, 64)), jnp.float32),
        "inner_weight": noise(splits[3], (INNER, INNER), INNER ** -0.5, 0.375),
        "outer_weight": noise(splits[4], (OUTER, OUTER), OUTER ** -0.5, 0.25),
        "position_diagonal_scaling": noise(splits[5], (OUTER, INNER), 1.0, 4.0, ((0, 64),), jnp.float32),
        "up_weight": noise(splits[6], (HID, BW), BW ** -0.5, 0.625, ((0, 8),)),
        "down_weight": noise(splits[7], (D, HB), HB ** -0.5, 0.3125, ((0, 8),)),
    }


finest_accuracy_setting = lax.Precision.HIGHEST

def gelu_slope(hidden):
    cumulative = 0.5 * (1.0 + lax.erf(hidden * (1.0 / math.sqrt(2.0))))
    density = jnp.exp(-0.5 * hidden * hidden) * (1.0 / math.sqrt(2.0 * math.pi))
    return cumulative + hidden * density

def rounded(values):
    return lax.optimization_barrier(values.astype(jnp.bfloat16)).astype(jnp.float32)

def reference(inputs, cotangent, kernel, inner_weight, outer_weight, position_diagonal_scaling, up_weight, down_weight):
    middle_full_operator = inner_weight.astype(jnp.float32)
    outer_full = outer_weight.astype(jnp.float32)
    block_width = D // NBLK
    block_hidden = HID // NBLK
    slice_rows = block_hidden // NBLK
    chan_x = inputs.reshape(NBLK, block_width, OUTER, INNER)
    chan_k = kernel.reshape(NBLK, block_width, INNER, OUTER)

    def forward_mix(pieces):
        channel_block, kernel_block = pieces
        leading_section = jnp.einsum('pb,cab->cap', middle_full_operator, channel_block, precision=finest_accuracy_setting)
        spectrum = jnp.einsum('pa,cab->cbp', outer_full, position_diagonal_scaling * leading_section, precision=finest_accuracy_setting)
        yielded_result_array = jnp.einsum('pa,cbp->cba', outer_full, kernel_block * spectrum, precision=finest_accuracy_setting)
        return jnp.einsum('wf,xwk->xkf', middle_full_operator, position_diagonal_scaling.T * yielded_result_array, precision=finest_accuracy_setting)
    mixing = lax.map(forward_mix, (chan_x, chan_k)).reshape(D, SEQ)
    pieces_count = 16
    token_span = SEQ // pieces_count

    def split_tokens(array):
        return jnp.moveaxis(array.reshape(D, pieces_count, token_span), 1, 0)
    up_blocks = up_weight.astype(jnp.float32).reshape(NBLK, block_hidden, block_width)
    down_blocks = down_weight.astype(jnp.float32).reshape(NBLK, block_width, NBLK, slice_rows)

    def channel_step(totals, pieces):
        total_up, total_down = totals
        channel_block, mix_block, adjoint_piece = pieces
        gated_full = channel_block + channel_block * mix_block
        gated_low = rounded(gated_full).reshape(NBLK, block_width, token_span)
        hidden = jnp.einsum('jrc,jct->jrt', up_blocks, gated_low, precision=finest_accuracy_setting)
        activation = rounded(jax.nn.gelu(hidden, approximate=False)).reshape(NBLK, NBLK, slice_rows, token_span)
        cot_low = rounded(adjoint_piece).reshape(NBLK, block_width, token_span)
        total_down = total_down + jnp.einsum('pot,jpqt->pojq', cot_low, activation, precision=finest_accuracy_setting)
        grad_act = rounded(jnp.einsum('pojq,pot->jpqt', down_blocks, cot_low, precision=finest_accuracy_setting))
        grad_act = grad_act.reshape(NBLK, block_hidden, token_span)
        grad_hidden = rounded(grad_act * gelu_slope(hidden))
        total_up = total_up + jnp.einsum('jrt,jct->jrc', grad_hidden, gated_low, precision=finest_accuracy_setting)
        grad_gated = adjoint_piece + jnp.einsum('jrc,jrt->jct', up_blocks, grad_hidden, precision=finest_accuracy_setting).reshape(D, token_span)
        return ((total_up, total_down), grad_gated)
    start = (jnp.zeros((NBLK, block_hidden, block_width), jnp.float32), jnp.zeros((NBLK, block_width, NBLK, slice_rows), jnp.float32))
    (sums_up, sums_down), grad_pieces = lax.scan(channel_step, start, (split_tokens(inputs), split_tokens(mixing), split_tokens(cotangent)))
    grad_gated = jnp.moveaxis(grad_pieces, 0, 1).reshape(D, SEQ)
    chan_g = grad_gated.reshape(NBLK, block_width, OUTER, INNER)
    chan_m = mixing.reshape(NBLK, block_width, OUTER, INNER)

    def backward_mix(pieces):
        channel_block, kernel_block, slope_piece, mix_block = pieces
        leading_section = jnp.einsum('pb,cab->cap', middle_full_operator, channel_block, precision=finest_accuracy_setting)
        spectrum = jnp.einsum('pa,cab->cbp', outer_full, position_diagonal_scaling * leading_section, precision=finest_accuracy_setting)
        yielded_result_array = jnp.einsum('pa,cbp->cba', outer_full, kernel_block * spectrum, precision=finest_accuracy_setting)
        grad_mix = slope_piece * channel_block
        second_factor = jnp.einsum('pb,cab->cap', middle_full_operator, grad_mix, precision=finest_accuracy_setting)
        grad_spec = jnp.einsum('pa,cab->cbp', outer_full, position_diagonal_scaling * second_factor, precision=finest_accuracy_setting)
        sensitivity_yielded_lines = jnp.einsum('pa,cbp->cba', outer_full, kernel_block * grad_spec, precision=finest_accuracy_setting)
        sensitivity_front_operand = jnp.einsum('wf,xwk->xkf', middle_full_operator, position_diagonal_scaling.T * sensitivity_yielded_lines, precision=finest_accuracy_setting)
        rotation_term = jnp.einsum('ekv,evk->vk', sensitivity_yielded_lines, leading_section, precision=finest_accuracy_setting) + jnp.einsum('xuk,xku->uk', second_factor, yielded_result_array, precision=finest_accuracy_setting)
        return (slope_piece * (1.0 + mix_block) + sensitivity_front_operand, grad_spec * spectrum, rotation_term)
    grad_in, grad_ker, twiddle_terms = lax.map(backward_mix, (chan_x, chan_k, chan_g, chan_m))
    grad_scale = 1.0 / math.sqrt(SEQ)
    return (grad_in.reshape(D, SEQ), grad_ker.reshape(D, INNER, OUTER), sums_up.reshape(HID, block_width) * grad_scale, sums_down.reshape(D, block_hidden) * grad_scale, lax.optimization_barrier(jnp.sum(twiddle_terms, axis=0)) * (1.0 / math.sqrt(D)))
```

```python
import functools
import math

import jax
import jax.numpy as jnp
from jax import lax
from jax.experimental import pallas as pl
from jax.experimental.pallas import tpu as pltpu
from jax.sharding import PartitionSpec as P

D = 768
HID = 3072
NBLK = 8
OUTER = 512
INNER = 256
SEQ = 131072
BW = D // NBLK
HB = HID // NBLK
SLICE = HB // NBLK
NSEQ = 64
ROWS = OUTER // NSEQ
COLS = INNER // NSEQ
LANES = COLS * BW
TOK = ROWS * INNER
LANE_TILE = 128

f32 = jnp.float32
bf16 = jnp.bfloat16
NT = (((1,), (1,)), ((), ()))
NN = (((1,), (0,)), ((), ()))


def dot(lhs, rhs, dims=NN):
    return lax.dot_general(lhs, rhs, dims, preferred_element_type=f32)


def call(kernel, outs, *operands, flops=0, scratch=(), trans=0):
    shapes = [jax.ShapeDtypeStruct(shape, dtype) for shape, dtype in outs]
    nbytes = sum(math.prod(o.shape) * o.dtype.itemsize for o in list(operands) + shapes)
    return pl.pallas_call(
        kernel,
        out_shape=shapes,
        in_specs=[pl.BlockSpec(memory_space=pltpu.VMEM)] * len(operands),
        out_specs=[pl.BlockSpec(memory_space=pltpu.VMEM)] * len(shapes),
        scratch_shapes=list(scratch),
        cost_estimate=pl.CostEstimate(flops=flops, bytes_accessed=nbytes, transcendentals=trans),
        compiler_params=pltpu.CompilerParams(vmem_limit_bytes=40 * 1024 * 1024),
    )(*operands)


def token_columns(a):
    return slice(a * INNER, (a + 1) * INNER)


def to_message(value, a, turned, stage):
    turned[:, :BW] = value.T
    parts = [turned[pl.ds(b, NSEQ, stride=COLS), :][:, :BW] for b in range(COLS)]
    row = jnp.concatenate(parts, axis=1)
    for k in range(LANES // LANE_TILE):
        stage[k, pl.ds(a, NSEQ, stride=ROWS), :] = row[:, k * LANE_TILE : (k + 1) * LANE_TILE]


def from_message(a, turned, stage):
    row = jnp.concatenate(
        [stage[k, pl.ds(a, NSEQ, stride=ROWS), :] for k in range(LANES // LANE_TILE)], axis=1
    )
    for b in range(COLS):
        turned[pl.ds(b, NSEQ, stride=COLS), :] = jnp.concatenate(
            [row[:, b * BW : (b + 1) * BW], jnp.zeros((NSEQ, LANE_TILE - BW), f32)], axis=1
        )
    return turned[...].T[:BW]


def pack(stage, send_ref):
    for k in range(LANES // LANE_TILE):
        send_ref[:, k * LANE_TILE : (k + 1) * LANE_TILE] = stage[k].astype(bf16)


def unpack(recv_ref, stage):
    for k in range(LANES // LANE_TILE):
        stage[k] = recv_ref[:, k * LANE_TILE : (k + 1) * LANE_TILE].astype(f32)


STAGE = pltpu.VMEM((LANES // LANE_TILE, OUTER, LANE_TILE), f32)
TURNED = pltpu.VMEM((INNER, LANE_TILE), f32)


def rows_in(x_ref, w_ref, tw_ref, send_ref, first_ref, turned, stage):
    w = w_ref[...]
    for a in range(ROWS):
        cols = token_columns(a)
        first = dot(x_ref[:, cols].astype(bf16), w, NT)
        first_ref[:, cols] = first.astype(bf16)
        to_message(first * tw_ref[a : a + 1, :], a, turned, stage)
    pack(stage, send_ref)


def columns(recv_ref, outer_ref, outer_t_ref, kernel_ref, send_ref, spec_ref):
    spec = dot(outer_ref[...], recv_ref[...])
    spec_ref[...] = spec.astype(spec_ref.dtype)
    scaled = (kernel_ref[...].astype(f32) * spec).astype(bf16)
    send_ref[...] = dot(outer_t_ref[...], scaled).astype(bf16)


def mlp(
    recv_ref,
    x_ref,
    cot_ref,
    grad_act_ref,
    w_ref,
    tw_ref,
    up_ref,
    up_t_ref,
    send_ref,
    back_ref,
    low_ref,
    act_ref,
    grad_hidden_ref,
    grad_mix_ref,
    direct_ref,
    turned,
    stage,
    turned_out,
    stage_out,
):
    unpack(recv_ref, stage)
    w = w_ref[...]
    up = up_ref[...]
    up_t = up_t_ref[...]
    for a in range(ROWS):
        cols = token_columns(a)
        twiddle = tw_ref[a : a + 1, :]
        back = from_message(a, turned, stage)
        back_ref[:, cols] = back.astype(bf16)
        mixing = dot((back * twiddle).astype(bf16), w)
        x = x_ref[:, cols]
        low = (x + x * mixing).astype(bf16)
        low_ref[:, cols] = low
        hidden = dot(up, low)
        cumulative = 0.5 * (1.0 + lax.erf(hidden * (1.0 / math.sqrt(2.0))))
        density = jnp.exp(-0.5 * hidden * hidden) * (1.0 / math.sqrt(2.0 * math.pi))
        act_ref[:, cols] = (hidden * cumulative).astype(bf16)
        slope = cumulative + hidden * density
        grad_hidden = (grad_act_ref[:, cols].astype(f32) * slope).astype(bf16)
        grad_hidden_ref[:, cols] = grad_hidden
        grad_gated = cot_ref[:, cols] + dot(up_t, grad_hidden)
        direct_ref[:, cols] = grad_gated * (1.0 + mixing)
        grad_mix = (grad_gated * x).astype(bf16)
        grad_mix_ref[:, cols] = grad_mix
        second = dot(grad_mix, w, NT)
        to_message(second * twiddle, a, turned_out, stage_out)
    pack(stage_out, send_ref)


def hidden_cotangent(shared_ref, out_ref):
    for p in range(NBLK):
        down = shared_ref[p, :, TOK : TOK + LANE_TILE].astype(f32).T[:SLICE].astype(bf16)
        out_ref[p * SLICE : (p + 1) * SLICE, :] = dot(down, shared_ref[p, :, :TOK]).astype(bf16)


def weight_grads(
    grad_hidden_ref, low_ref, act_ref, shared_ref, grad_mix_ref, back_ref, w_ref, up_ref, down_ref, later_ref
):
    zeros = jnp.zeros((HB, LANE_TILE - BW), f32)
    up_ref[...] = jnp.concatenate([dot(grad_hidden_ref[...], low_ref[...], NT), zeros], axis=1).astype(bf16)
    for p in range(NBLK):
        rows = slice(p * SLICE, (p + 1) * SLICE)
        part = dot(act_ref[rows, :], shared_ref[p, :, :TOK], NT)
        down_ref[rows, :] = jnp.concatenate([part, zeros[:SLICE]], axis=1).astype(bf16)
    w = w_ref[...]
    for a in range(ROWS):
        cols = token_columns(a)
        second = dot(grad_mix_ref[:, cols], w, NT)
        later_ref[a : a + 1, :] = jnp.sum(second * back_ref[:, cols].astype(f32), axis=0, keepdims=True)


def rows_out(recv_ref, w_ref, tw_ref, first_ref, direct_ref, later_ref, out_ref, twiddle_ref, turned, stage):
    unpack(recv_ref, stage)
    w = w_ref[...]
    for a in range(ROWS):
        cols = token_columns(a)
        grad_back = from_message(a, turned, stage)
        early = jnp.sum(grad_back * first_ref[:, cols].astype(f32), axis=0, keepdims=True)
        twiddle_ref[a : a + 1, :] = early + later_ref[a : a + 1, :]
        out_ref[:, cols] = direct_ref[:, cols] + dot((grad_back * tw_ref[a : a + 1, :]).astype(bf16), w)


def exchange(values):
    return lax.all_to_all(
        values.reshape(NSEQ, ROWS, LANES), "seq", split_axis=0, concat_axis=0, tiled=True
    ).reshape(OUTER, LANES)


def to_all(value, axis, size):
    copies = jnp.broadcast_to(value[None], (size,) + value.shape)
    return lax.all_to_all(copies, axis, split_axis=0, concat_axis=0, tiled=True)


def on_device(inputs, cotangent, kernel, inner_weight, outer_weight, twiddle, up_weight, down_weight):
    mix_flops = 2 * BW * TOK * INNER
    col_flops = 4 * OUTER * OUTER * LANES
    mlp_flops = 2 * HB * BW * TOK

    send, first = call(
        rows_in,
        [((OUTER, LANES), bf16), ((BW, TOK), bf16)],
        inputs,
        inner_weight,
        twiddle,
        flops=mix_flops,
        scratch=[TURNED, STAGE],
    )

    cotangent_late, down_late, send = lax.optimization_barrier((cotangent, down_weight, send))
    down_parts = down_late.reshape(BW, NBLK, SLICE).transpose(1, 0, 2)
    down_parts = jnp.pad(down_parts, ((0, 0), (0, 0), (0, LANE_TILE - SLICE)))
    cot_parts = jnp.broadcast_to(cotangent_late.astype(bf16)[None], (NBLK, BW, TOK))
    shared = lax.all_to_all(
        jnp.concatenate([cot_parts, down_parts], axis=2), "chan", split_axis=0, concat_axis=0, tiled=True
    )

    kernel_t = kernel.astype(bf16).transpose(2, 1, 0).reshape(OUTER, LANES)
    outer_t = outer_weight.T
    up_t = up_weight.T

    recv = exchange(send)
    send, spectrum = call(
        columns,
        [((OUTER, LANES), bf16), ((OUTER, LANES), bf16)],
        recv,
        outer_weight,
        outer_t,
        kernel_t,
        flops=col_flops,
    )
    recv = exchange(send)
    (grad_act,) = call(hidden_cotangent, [((HB, TOK), bf16)], shared, flops=mlp_flops)
    send, back, low, act, grad_hidden, grad_mix, direct = call(
        mlp,
        [
            ((OUTER, LANES), bf16),
            ((BW, TOK), bf16),
            ((BW, TOK), bf16),
            ((HB, TOK), bf16),
            ((HB, TOK), bf16),
            ((BW, TOK), bf16),
            ((BW, TOK), f32),
        ],
        recv,
        inputs,
        cotangent,
        grad_act,
        inner_weight,
        twiddle,
        up_weight,
        up_t,
        flops=2 * mix_flops + 2 * mlp_flops,
        trans=2 * HB * TOK,
        scratch=[TURNED, STAGE, TURNED, STAGE],
    )
    recv = exchange(send)

    up_part, down_part, later = call(
        weight_grads,
        [((HB, LANE_TILE), bf16), ((HB, LANE_TILE), bf16), ((ROWS, INNER), f32)],
        grad_hidden,
        low,
        act,
        shared,
        grad_mix,
        back,
        inner_weight,
        flops=2 * mlp_flops + mix_flops,
    )
    down_part = lax.all_to_all(
        down_part.reshape(NBLK, SLICE, LANE_TILE), "chan", split_axis=0, concat_axis=0, tiled=True
    ).reshape(HB, LANE_TILE)
    share = 16
    grads = jnp.concatenate(
        [up_part, down_part, jnp.zeros((NSEQ * share - 2 * HB, LANE_TILE), bf16)], axis=0
    ).reshape(NSEQ, share, LANE_TILE)
    grads = lax.all_to_all(grads, "seq", split_axis=0, concat_axis=0, tiled=True)
    grads = jnp.sum(grads.astype(f32), axis=0) * (1.0 / math.sqrt(SEQ))
    grads = to_all(grads.astype(bf16), "seq", NSEQ).reshape(NSEQ * share, LANE_TILE).astype(f32)
    grad_up = grads[:HB, :BW]
    grad_down = grads[HB : 2 * HB, :BW].T

    send, grad_spec = call(
        columns,
        [((OUTER, LANES), bf16), ((OUTER, LANES), f32)],
        recv,
        outer_weight,
        outer_t,
        kernel_t,
        flops=col_flops,
    )
    recv = exchange(send)
    grad_kernel = (grad_spec * spectrum.astype(f32)).reshape(OUTER, COLS, BW).transpose(2, 1, 0)

    grad_inputs, grad_twiddle = call(
        rows_out,
        [((BW, TOK), f32), ((ROWS, INNER), f32)],
        recv,
        inner_weight,
        twiddle,
        first,
        direct,
        later,
        flops=mix_flops,
        scratch=[TURNED, STAGE],
    )
    grad_twiddle = jnp.sum(to_all(grad_twiddle, "chan", NBLK), axis=0) * (1.0 / math.sqrt(D))
    return grad_inputs, grad_kernel, grad_up, grad_down, grad_twiddle


def solution(mesh):
    placed = (
        P("chan", "seq"),
        P("chan", "seq"),
        P("chan", "seq", None),
        P(),
        P(),
        P("seq", None),
        P("chan", None),
        P("chan", None),
    )
    return jax.shard_map(
        on_device,
        mesh=mesh,
        in_specs=placed,
        out_specs=(
            P("chan", "seq"),
            P("chan", "seq", None),
            P("chan", None),
            P("chan", None),
            P("seq", None),
        ),
        check_vma=False,
    )
```

```python
import functools
import math

import jax
import jax.numpy as jnp
from jax import lax
from jax.experimental import pallas as pl
from jax.experimental.pallas import tpu as pltpu
from jax.sharding import PartitionSpec as P

D = 768
HID = 3072
NBLK = 8
OUTER = 512
INNER = 256
SEQ = 131072
BW = D // NBLK
HB = HID // NBLK
SLICE = HB // NBLK
NSEQ = 64
ROWS = OUTER // NSEQ
COLS = INNER // NSEQ
LANES = COLS * BW
TOK = ROWS * INNER
LANE_TILE = 128
WIDE = LANES + 2 * LANE_TILE

f32 = jnp.float32
bf16 = jnp.bfloat16
NT = (((1,), (1,)), ((), ()))
NN = (((1,), (0,)), ((), ()))


def dot(lhs, rhs, dims=NN):
    return lax.dot_general(lhs, rhs, dims, preferred_element_type=f32)


class Stacked:
    def __init__(self, parts, shape, places):
        self.parts, self.shape, self.places = parts, shape, places
        self.dtype = parts[0].dtype


def call(body, outs, *operands, flops=0, scratch=(), trans=0):
    shapes = [jax.ShapeDtypeStruct(shape, dtype) for shape, dtype in outs]
    nbytes = sum(math.prod(o.shape) * o.dtype.itemsize for o in list(operands) + shapes)
    arrays = []
    for operand in operands:
        arrays += operand.parts if isinstance(operand, Stacked) else [operand]
    n_in, n_out = len(operands), len(shapes)

    def kernel(*refs):
        sources, targets, refs = refs[: len(arrays)], refs[len(arrays) : len(arrays) + n_out], refs[len(arrays) + n_out :]
        held, built, refs = refs[:n_in], refs[n_in : n_in + n_out], refs[n_in + n_out :]
        in_sems, out_sems, refs = refs[0], refs[1], refs[2:]
        loads, taken = [], 0
        for operand, ref in zip(operands, held):
            if isinstance(operand, Stacked):
                places = operand.places(ref)
            else:
                places = [ref]
            copies = []
            for place in places:
                copies.append(pltpu.make_async_copy(sources[taken], place, in_sems.at[taken]))
                copies[-1].start()
                taken += 1
            loads.append(copies)

        def ready(i):
            while loads[i]:
                loads[i].pop().wait()
            return held[i]

        stores = []

        class Out:
            def __init__(self, i):
                self.i, self.ref, self.parts = i, built[i], 0

            def store(self, *index):
                source = built[self.i].at[index] if index else built[self.i]
                target = targets[self.i].at[index] if index else targets[self.i]
                copy = pltpu.make_async_copy(source, target, out_sems.at[self.i, self.parts])
                self.parts += 1
                copy.start()
                stores.append(copy)

        out = [Out(i) for i in range(n_out)]
        body([functools.partial(ready, i) for i in range(n_in)], out, *refs)
        for i in range(n_in):
            ready(i)
        for o in out:
            if not o.parts:
                o.store()
        for copy in stores:
            copy.wait()

    return pl.pallas_call(
        kernel,
        out_shape=shapes,
        in_specs=[pl.BlockSpec(memory_space=pltpu.HBM)] * len(arrays),
        out_specs=[pl.BlockSpec(memory_space=pltpu.HBM)] * n_out,
        scratch_shapes=[pltpu.VMEM(o.shape, o.dtype) for o in list(operands) + shapes]
        + [pltpu.SemaphoreType.DMA((len(arrays),)), pltpu.SemaphoreType.DMA((n_out, ROWS))]
        + list(scratch),
        cost_estimate=pl.CostEstimate(flops=flops, bytes_accessed=nbytes, transcendentals=trans),
        compiler_params=pltpu.CompilerParams(vmem_limit_bytes=60 * 1024 * 1024),
    )(*arrays)


def token_columns(a):
    return slice(a * INNER, (a + 1) * INNER)


def to_message(value, a, turned, stage):
    turned[:, :BW] = value.T
    parts = [turned[pl.ds(b, NSEQ, stride=COLS), :][:, :BW] for b in range(COLS)]
    row = jnp.concatenate(parts, axis=1)
    for k in range(LANES // LANE_TILE):
        stage[k, pl.ds(a, NSEQ, stride=ROWS), :] = row[:, k * LANE_TILE : (k + 1) * LANE_TILE]


def from_message(a, turned, stage):
    row = jnp.concatenate(
        [stage[k, pl.ds(a, NSEQ, stride=ROWS), :] for k in range(LANES // LANE_TILE)], axis=1
    )
    for b in range(COLS):
        turned[pl.ds(b, NSEQ, stride=COLS), :] = jnp.concatenate(
            [row[:, b * BW : (b + 1) * BW], jnp.zeros((NSEQ, LANE_TILE - BW), f32)], axis=1
        )
    return turned[...].T[:BW]


def pack(stage, send_ref):
    for k in range(LANES // LANE_TILE):
        send_ref[:, k * LANE_TILE : (k + 1) * LANE_TILE] = stage[k].astype(bf16)


def unpack(recv_ref, stage):
    for k in range(LANES // LANE_TILE):
        stage[k] = recv_ref[:, k * LANE_TILE : (k + 1) * LANE_TILE].astype(f32)


STAGE = pltpu.VMEM((LANES // LANE_TILE, OUTER, LANE_TILE), f32)
TURNED = pltpu.VMEM((INNER, LANE_TILE), f32)


def rows_in(ins, outs, turned, stage):
    x, w, twiddle = ins
    send, first_out = outs
    for a in range(ROWS):
        cols = token_columns(a)
        first = dot(x()[:, cols].astype(bf16), w()[...], NT)
        first_out.ref[:, cols] = first.astype(bf16)
        to_message(first * twiddle()[a : a + 1, :], a, turned, stage)
    first_out.store()
    pack(stage, send.ref)


def columns(ins, outs):
    recv, outer, kernel, outer_t = ins
    send, spec_out = outs
    spec = dot(outer()[...], recv()[:, :LANES])
    spec_out.ref[...] = spec.astype(spec_out.ref.dtype)
    spec_out.store()
    scaled = (kernel()[...].astype(f32) * spec).astype(bf16)
    send.ref[:, :LANES] = dot(outer_t()[...], scaled).astype(bf16)
    if recv().shape[1] == WIDE:
        parts = recv()[:, LANES:].astype(f32).reshape(NSEQ, ROWS, WIDE - LANES)
        total = jnp.sum(parts, axis=0, keepdims=True)
        send.ref[:, LANES:] = (
            jnp.broadcast_to(total, parts.shape).reshape(OUTER, WIDE - LANES).astype(bf16)
        )


def mlp(ins, outs, turned, stage, turned_out, stage_out, down_t, down_own, grad_up, grad_down):
    recv, w, twiddle, x_in, up, shared, up_t, cot = ins
    send, later, direct = outs
    me = lax.axis_index("chan")
    unpack(recv(), stage)
    for a in range(ROWS):
        cols = token_columns(a)
        scale = twiddle()[a : a + 1, :]
        back = from_message(a, turned, stage)
        mixing = dot((back * scale).astype(bf16), w()[...])
        x = x_in()[:, cols]
        low = (x + x * mixing).astype(bf16)
        hidden = dot(up()[...], low)
        cumulative = 0.5 * (1.0 + lax.erf(hidden * (1.0 / math.sqrt(2.0))))
        density = jnp.exp(-0.5 * hidden * hidden) * (1.0 / math.sqrt(2.0 * math.pi))
        act = (hidden * cumulative).astype(bf16)
        slope = cumulative + hidden * density
        if a == 0:
            for p in range(NBLK):
                down_t[...] = shared()[p, :, TOK:].astype(f32).T
                own = pl.ds(pl.multiple_of(me * SLICE, SLICE), SLICE)
                down_own[p * SLICE : (p + 1) * SLICE, :] = down_t[own, :].astype(bf16)
        grad_act, down_part = [], []
        for p in range(NBLK):
            rows = slice(p * SLICE, (p + 1) * SLICE)
            cot_low = shared()[p, :, cols]
            grad_act.append(dot(down_own[rows, :], cot_low).astype(bf16))
            down_part.append(dot(act[rows], cot_low, NT))
        grad_act = jnp.concatenate(grad_act, axis=0).astype(f32)
        down_part = jnp.concatenate(down_part, axis=0)
        grad_hidden = (grad_act * slope).astype(bf16)
        up_part = dot(grad_hidden, low, NT)
        if a == 0:
            grad_up[...] = up_part
            grad_down[...] = down_part
        else:
            grad_up[...] += up_part
            grad_down[...] += down_part
        grad_gated = cot()[:, cols] + dot(up_t()[...], grad_hidden)
        direct.ref[:, cols] = grad_gated * (1.0 + mixing)
        direct.store(slice(None), cols)
        grad_mix = (grad_gated * x).astype(bf16)
        second = dot(grad_mix, w()[...], NT)
        later.ref[a : a + 1, :] = jnp.sum(second * back, axis=0, keepdims=True)
        to_message(second * scale, a, turned_out, stage_out)
    pack(stage_out, send.ref)
    zeros = jnp.zeros((HB, LANE_TILE - BW), f32)
    for start, total in ((LANES, grad_up), (LANES + LANE_TILE, grad_down)):
        send.ref[:HB, start : start + LANE_TILE] = jnp.concatenate([total[...], zeros], axis=1).astype(bf16)
    send.ref[HB:, LANES:] = jnp.zeros((OUTER - HB, WIDE - LANES), bf16)


def gather_over_chan(block):
    across, left, right, far = (lax.ppermute(block, "chan", step_to(step)) for step in ((1, 0), (0, 1), (0, 3), (1, 2)))
    half = BW // 2

    def onward():
        return (
            lax.ppermute(across, "chan", step_to((0, 1))),
            lax.ppermute(across, "chan", step_to((0, 3))),
            lax.ppermute(left[:half], "chan", step_to((0, 1))),
            lax.ppermute(right[half:], "chan", step_to((0, 3))),
        )

    return (across, left, right, far), onward


def block_places(ref):
    me = lax.axis_index("chan")
    half = BW // 2

    def at(dy, dx):
        return ref.at[(me // 4 + dy) % 2 * 4 + (me % 4 + dx) % 4]

    opposite = at(0, 2)
    return [
        at(0, 0),
        at(1, 0),
        at(0, 3),
        at(0, 1),
        at(1, 2),
        at(1, 3),
        at(1, 1),
        opposite.at[pl.ds(0, half)],
        opposite.at[pl.ds(half, half)],
    ]


def twiddle_terms(ins, outs, turned, stage):
    recv, first, later, twiddle = ins
    shared, grad_back_out, grad_up = outs
    grad_up.ref[...] = recv()[:HB, LANES : LANES + BW].astype(f32) * (1.0 / math.sqrt(SEQ))
    grad_up.store()
    unpack(recv(), stage)
    terms = []
    for a in range(ROWS):
        cols = token_columns(a)
        grad_back = from_message(a, turned, stage)
        terms.append(
            jnp.sum(grad_back * first()[:, cols].astype(f32), axis=0, keepdims=True) + later()[a : a + 1, :]
        )
        grad_back_out.ref[:, cols] = (grad_back * twiddle()[a : a + 1, :]).astype(bf16)
    grad_back_out.store()
    terms = jnp.concatenate(terms, axis=0)
    terms = jnp.concatenate([terms[:, :LANE_TILE], terms[:, LANE_TILE:]], axis=0).astype(bf16)
    for p in range(NBLK):
        shared.ref[p, :SLICE, :] = recv()[p * SLICE : (p + 1) * SLICE, LANES + LANE_TILE :]
        shared.ref[p, SLICE:, :] = terms


def rows_out(ins, outs):
    grad_back, w, direct = ins
    (out,) = outs
    for a in range(ROWS):
        cols = token_columns(a)
        out.ref[:, cols] = direct()[:, cols] + dot(grad_back()[:, cols], w()[...])
        out.store(slice(None), cols)


def finish(ins, outs):
    (shared,) = ins
    grad_down, grad_twiddle = outs
    terms = jnp.sum(shared()[:, SLICE:, :].astype(f32), axis=0) * (1.0 / math.sqrt(D))
    grad_twiddle.ref[:, :LANE_TILE] = terms[:ROWS]
    grad_twiddle.ref[:, LANE_TILE:] = terms[ROWS:]
    down = jnp.concatenate([shared()[j, :SLICE, :].astype(f32) for j in range(NBLK)], axis=0)
    grad_down.ref[...] = down.T[:BW] * (1.0 / math.sqrt(SEQ))


def exchange(values):
    return lax.all_to_all(
        values.reshape(NSEQ, ROWS, -1), "seq", split_axis=0, concat_axis=0, tiled=True
    ).reshape(values.shape)


def step_to(step):
    dy, dx = step
    return [(y * 4 + x, (y + dy) % 2 * 4 + (x + dx) % 4) for y in range(2) for x in range(4)]


def on_device(inputs, cotangent, kernel, inner_weight, outer_weight, twiddle, up_weight, down_weight):
    mix_flops = 2 * BW * TOK * INNER
    col_flops = 4 * OUTER * OUTER * LANES
    mlp_flops = 2 * HB * BW * TOK
    send, first = call(
        rows_in,
        [((OUTER, LANES), bf16), ((BW, TOK), bf16)],
        inputs,
        inner_weight,
        twiddle,
        flops=mix_flops,
        scratch=[TURNED, STAGE],
    )

    cotangent_late, down_late, send = lax.optimization_barrier((cotangent, down_weight, send))
    block = jnp.concatenate([cotangent_late.astype(bf16), down_late], axis=1)
    straight, onward = gather_over_chan(block)
    shared = (block,) + straight + onward()
    shared = Stacked(shared, (NBLK, BW, TOK + HB), block_places)

    kernel_t = kernel.astype(bf16).transpose(2, 1, 0).reshape(OUTER, LANES)
    outer_t = outer_weight.T
    up_t = up_weight.T

    recv, *straight = lax.optimization_barrier((exchange(send),) + straight)
    send, spectrum = call(
        columns,
        [((OUTER, LANES), bf16), ((OUTER, LANES), bf16)],
        recv,
        outer_weight,
        kernel_t,
        outer_t,
        flops=col_flops,
    )
    recv = exchange(send)
    send, later, direct = call(
        mlp,
        [((OUTER, WIDE), bf16), ((ROWS, INNER), f32), ((BW, TOK), f32)],
        recv,
        inner_weight,
        twiddle,
        inputs,
        up_weight,
        shared,
        up_t,
        cotangent,
        flops=2 * mix_flops + 5 * mlp_flops,
        trans=2 * HB * TOK,
        scratch=[
            TURNED,
            STAGE,
            TURNED,
            STAGE,
            pltpu.VMEM((HB, BW), f32),
            pltpu.VMEM((HB, BW), bf16),
            pltpu.VMEM((HB, BW), f32),
            pltpu.VMEM((HB, BW), f32),
        ],
    )
    recv = exchange(send)

    send, grad_spec = call(
        columns,
        [((OUTER, WIDE), bf16), ((OUTER, LANES), f32)],
        recv,
        outer_weight,
        kernel_t,
        outer_t,
        flops=col_flops,
    )
    recv = exchange(send)
    grad_kernel = (grad_spec * spectrum.astype(f32)).reshape(OUTER, COLS, BW).transpose(2, 1, 0)

    shared, grad_back, grad_up = call(
        twiddle_terms,
        [((NBLK, SLICE + 2 * ROWS, LANE_TILE), bf16), ((BW, TOK), bf16), ((HB, BW), f32)],
        recv,
        first,
        later,
        twiddle,
        scratch=[TURNED, STAGE],
    )
    shared = lax.all_to_all(shared, "chan", split_axis=0, concat_axis=0, tiled=True)
    (grad_inputs,) = call(
        rows_out, [((BW, TOK), f32)], grad_back, inner_weight, direct, flops=mix_flops
    )
    grad_down, grad_twiddle = call(finish, [((BW, HB), f32), ((ROWS, INNER), f32)], shared)
    return grad_inputs, grad_kernel, grad_up, grad_down, grad_twiddle


def solution(mesh):
    placed = (
        P("chan", "seq"),
        P("chan", "seq"),
        P("chan", "seq", None),
        P(),
        P(),
        P("seq", None),
        P("chan", None),
        P("chan", None),
    )
    return jax.shard_map(
        on_device,
        mesh=mesh,
        in_specs=placed,
        out_specs=(
            P("chan", "seq"),
            P("chan", "seq", None),
            P("chan", None),
            P("chan", None),
            P("seq", None),
        ),
        check_vma=False,
    )
```

```python
import functools
import math

import jax
import jax.numpy as jnp
from jax import lax
from jax.experimental import pallas as pl
from jax.experimental.pallas import tpu as pltpu
from jax.sharding import PartitionSpec as P

D = 768
HID = 3072
NBLK = 8
OUTER = 512
INNER = 256
SEQ = 131072
BW = D // NBLK
HB = HID // NBLK
SLICE = HB // NBLK
NSEQ = 64
ROWS = OUTER // NSEQ
COLS = INNER // NSEQ
LANES = COLS * BW
TOK = ROWS * INNER
LANE_TILE = 128
WIDE = LANES + 2 * LANE_TILE

f32 = jnp.float32
bf16 = jnp.bfloat16
NT = (((1,), (1,)), ((), ()))
NN = (((1,), (0,)), ((), ()))


def dot(lhs, rhs, dims=NN):
    return lax.dot_general(lhs, rhs, dims, preferred_element_type=f32)


class Stacked:
    def __init__(self, parts, shape, places):
        self.parts, self.shape, self.places = parts, shape, places
        self.dtype = parts[0].dtype


def call(body, outs, *operands, flops=0, scratch=(), trans=0):
    shapes = [jax.ShapeDtypeStruct(shape, dtype) for shape, dtype in outs]
    nbytes = sum(math.prod(o.shape) * o.dtype.itemsize for o in list(operands) + shapes)
    arrays = []
    for operand in operands:
        arrays += list(operand.parts) if isinstance(operand, Stacked) else [operand]
    n_in, n_out = len(operands), len(shapes)

    def kernel(*refs):
        sources, targets, refs = refs[: len(arrays)], refs[len(arrays) : len(arrays) + n_out], refs[len(arrays) + n_out :]
        held, built, refs = refs[:n_in], refs[n_in : n_in + n_out], refs[n_in + n_out :]
        in_sems, out_sems, refs = refs[0], refs[1], refs[2:]
        loads, taken, n_copies = [], 0, 0
        for operand, ref in zip(operands, held):
            if isinstance(operand, Stacked):
                moves = [
                    (source.at[pl.ds(start, rows)], place)
                    for source, places in zip(sources[taken:], operand.places(ref))
                    for start, rows, place in places
                ]
                taken += len(operand.parts)
            else:
                moves = [(sources[taken], ref)]
                taken += 1
            copies = []
            for source, place in moves:
                copies.append(pltpu.make_async_copy(source, place, in_sems.at[n_copies]))
                copies[-1].start()
                n_copies += 1
            loads.append(copies)

        def ready(i):
            while loads[i]:
                loads[i].pop().wait()
            return held[i]

        stores = []

        class Out:
            def __init__(self, i):
                self.i, self.ref, self.parts = i, built[i], 0

            def store(self, *index):
                source = built[self.i].at[index] if index else built[self.i]
                target = targets[self.i].at[index] if index else targets[self.i]
                copy = pltpu.make_async_copy(source, target, out_sems.at[self.i, self.parts])
                self.parts += 1
                copy.start()
                stores.append(copy)

        out = [Out(i) for i in range(n_out)]
        body([functools.partial(ready, i) for i in range(n_in)], out, *refs)
        for i in range(n_in):
            ready(i)
        for o in out:
            if not o.parts:
                o.store()
        for copy in stores:
            copy.wait()

    return pl.pallas_call(
        kernel,
        out_shape=shapes,
        in_specs=[pl.BlockSpec(memory_space=pltpu.HBM)] * len(arrays),
        out_specs=[pl.BlockSpec(memory_space=pltpu.HBM)] * n_out,
        scratch_shapes=[pltpu.VMEM(o.shape, o.dtype) for o in list(operands) + shapes]
        + [pltpu.SemaphoreType.DMA((2 * len(arrays),)), pltpu.SemaphoreType.DMA((n_out, ROWS))]
        + list(scratch),
        cost_estimate=pl.CostEstimate(flops=flops, bytes_accessed=nbytes, transcendentals=trans),
        compiler_params=pltpu.CompilerParams(vmem_limit_bytes=60 * 1024 * 1024),
    )(*arrays)


def token_columns(a):
    return slice(a * INNER, (a + 1) * INNER)


def to_message(value, a, turned, stage):
    turned[:, :BW] = value.T
    parts = [turned[pl.ds(b, NSEQ, stride=COLS), :][:, :BW] for b in range(COLS)]
    row = jnp.concatenate(parts, axis=1)
    for k in range(LANES // LANE_TILE):
        stage[k, pl.ds(a, NSEQ, stride=ROWS), :] = row[:, k * LANE_TILE : (k + 1) * LANE_TILE]


def from_message(a, turned, stage):
    row = jnp.concatenate(
        [stage[k, pl.ds(a, NSEQ, stride=ROWS), :] for k in range(LANES // LANE_TILE)], axis=1
    )
    for b in range(COLS):
        turned[pl.ds(b, NSEQ, stride=COLS), :] = jnp.concatenate(
            [row[:, b * BW : (b + 1) * BW], jnp.zeros((NSEQ, LANE_TILE - BW), f32)], axis=1
        )
    return turned[...].T[:BW]


def pack(stage, send_ref):
    for k in range(LANES // LANE_TILE):
        send_ref[:, k * LANE_TILE : (k + 1) * LANE_TILE] = stage[k].astype(bf16)


def unpack(recv_ref, stage):
    for k in range(LANES // LANE_TILE):
        stage[k] = recv_ref[:, k * LANE_TILE : (k + 1) * LANE_TILE].astype(f32)


STAGE = pltpu.VMEM((LANES // LANE_TILE, OUTER, LANE_TILE), f32)
TURNED = pltpu.VMEM((INNER, LANE_TILE), f32)


def rows_in(ins, outs, turned, stage):
    x, w, twiddle = ins
    send, first_out = outs
    for a in range(ROWS):
        cols = token_columns(a)
        first = dot(x()[:, cols].astype(bf16), w()[...], NT)
        first_out.ref[:, cols] = first.astype(bf16)
        to_message(first * twiddle()[a : a + 1, :], a, turned, stage)
    first_out.store()
    pack(stage, send.ref)


def columns(ins, outs):
    recv, outer, kernel, outer_t = ins
    send, spec_out = outs
    spec = dot(outer()[...], recv()[:, :LANES])
    spec_out.ref[...] = spec.astype(spec_out.ref.dtype)
    spec_out.store()
    scaled = (kernel()[...].astype(f32) * spec).astype(bf16)
    send.ref[:, :LANES] = dot(outer_t()[...], scaled).astype(bf16)
    if recv().shape[1] == WIDE:
        parts = recv()[:, LANES:].astype(f32).reshape(NSEQ, ROWS, WIDE - LANES)
        total = jnp.sum(parts, axis=0, keepdims=True)
        send.ref[:, LANES:] = (
            jnp.broadcast_to(total, parts.shape).reshape(OUTER, WIDE - LANES).astype(bf16)
        )


def mlp(ins, outs, turned, stage, turned_out, stage_out, down_t, down_own, grad_up, grad_down):
    recv, w, twiddle, x_in, up, shared, up_t, cot = ins
    send, later, direct = outs
    me = lax.axis_index("chan")
    unpack(recv(), stage)
    for a in range(ROWS):
        cols = token_columns(a)
        scale = twiddle()[a : a + 1, :]
        back = from_message(a, turned, stage)
        mixing = dot((back * scale).astype(bf16), w()[...])
        x = x_in()[:, cols]
        low = (x + x * mixing).astype(bf16)
        hidden = dot(up()[...], low)
        cumulative = 0.5 * (1.0 + lax.erf(hidden * (1.0 / math.sqrt(2.0))))
        density = jnp.exp(-0.5 * hidden * hidden) * (1.0 / math.sqrt(2.0 * math.pi))
        act = (hidden * cumulative).astype(bf16)
        slope = cumulative + hidden * density
        if a == 0:
            for p in range(NBLK):
                down_t[...] = shared()[p, :, TOK:].astype(f32).T
                own = pl.ds(pl.multiple_of(me * SLICE, SLICE), SLICE)
                down_own[p * SLICE : (p + 1) * SLICE, :] = down_t[own, :].astype(bf16)
        grad_act, down_part = [], []
        for p in range(NBLK):
            rows = slice(p * SLICE, (p + 1) * SLICE)
            cot_low = shared()[p, :, cols]
            grad_act.append(dot(down_own[rows, :], cot_low).astype(bf16))
            down_part.append(dot(act[rows], cot_low, NT))
        grad_act = jnp.concatenate(grad_act, axis=0).astype(f32)
        down_part = jnp.concatenate(down_part, axis=0)
        grad_hidden = (grad_act * slope).astype(bf16)
        up_part = dot(grad_hidden, low, NT)
        if a == 0:
            grad_up[...] = up_part
            grad_down[...] = down_part
        else:
            grad_up[...] += up_part
            grad_down[...] += down_part
        grad_gated = cot()[:, cols] + dot(up_t()[...], grad_hidden)
        direct.ref[:, cols] = grad_gated * (1.0 + mixing)
        direct.store(slice(None), cols)
        grad_mix = (grad_gated * x).astype(bf16)
        second = dot(grad_mix, w()[...], NT)
        later.ref[a : a + 1, :] = jnp.sum(second * back, axis=0, keepdims=True)
        to_message(second * scale, a, turned_out, stage_out)
    pack(stage_out, send.ref)
    zeros = jnp.zeros((HB, LANE_TILE - BW), f32)
    for start, total in ((LANES, grad_up), (LANES + LANE_TILE, grad_down)):
        send.ref[:HB, start : start + LANE_TILE] = jnp.concatenate([total[...], zeros], axis=1).astype(bf16)
    send.ref[HB:, LANES:] = jnp.zeros((OUTER - HB, WIDE - LANES), bf16)


def gather_over_chan(block):
    straight = [lax.ppermute(block, "chan", step_to(step)) for step in ((1, 0), (0, 1), (0, 3), (1, 2))]
    across, left, right, far = lax.optimization_barrier(straight)
    half = BW // 2
    onward_left = lax.ppermute(jnp.concatenate([across, left[:half]]), "chan", step_to((0, 1)))
    onward_right = lax.ppermute(jnp.concatenate([across, right[half:]]), "chan", step_to((0, 3)))
    return block, across, left, right, far, onward_left, onward_right


def block_places(ref):
    me = lax.axis_index("chan")
    half = BW // 2

    def at(dy, dx):
        return ref.at[(me // 4 + dy) % 2 * 4 + (me % 4 + dx) % 4]

    return [
        [(0, BW, at(0, 0))],
        [(0, BW, at(1, 0))],
        [(0, BW, at(0, 3))],
        [(0, BW, at(0, 1))],
        [(0, BW, at(1, 2))],
        [(0, BW, at(1, 3)), (BW, half, at(0, 2).at[pl.ds(0, half)])],
        [(0, BW, at(1, 1)), (BW, half, at(0, 2).at[pl.ds(half, half)])],
    ]


def twiddle_terms(ins, outs, turned, stage):
    recv, first, later, twiddle = ins
    shared, grad_back_out, grad_up = outs
    grad_up.ref[...] = recv()[:HB, LANES : LANES + BW].astype(f32) * (1.0 / math.sqrt(SEQ))
    grad_up.store()
    unpack(recv(), stage)
    terms = []
    for a in range(ROWS):
        cols = token_columns(a)
        grad_back = from_message(a, turned, stage)
        terms.append(
            jnp.sum(grad_back * first()[:, cols].astype(f32), axis=0, keepdims=True) + later()[a : a + 1, :]
        )
        grad_back_out.ref[:, cols] = (grad_back * twiddle()[a : a + 1, :]).astype(bf16)
    grad_back_out.store()
    terms = jnp.concatenate(terms, axis=0)
    terms = jnp.concatenate([terms[:, :LANE_TILE], terms[:, LANE_TILE:]], axis=0).astype(bf16)
    for p in range(NBLK):
        shared.ref[p, :SLICE, :] = recv()[p * SLICE : (p + 1) * SLICE, LANES + LANE_TILE :]
        shared.ref[p, SLICE:, :] = terms


def rows_out(ins, outs):
    grad_back, w, direct = ins
    (out,) = outs
    for a in range(ROWS):
        cols = token_columns(a)
        out.ref[:, cols] = direct()[:, cols] + dot(grad_back()[:, cols], w()[...])
        out.store(slice(None), cols)


def finish(ins, outs):
    (shared,) = ins
    grad_down, grad_twiddle = outs
    terms = jnp.sum(shared()[:, SLICE:, :].astype(f32), axis=0) * (1.0 / math.sqrt(D))
    grad_twiddle.ref[:, :LANE_TILE] = terms[:ROWS]
    grad_twiddle.ref[:, LANE_TILE:] = terms[ROWS:]
    down = jnp.concatenate([shared()[j, :SLICE, :].astype(f32) for j in range(NBLK)], axis=0)
    grad_down.ref[...] = down.T[:BW] * (1.0 / math.sqrt(SEQ))


def exchange(values):
    return lax.all_to_all(
        values.reshape(NSEQ, ROWS, -1), "seq", split_axis=0, concat_axis=0, tiled=True
    ).reshape(values.shape)


def step_to(step):
    dy, dx = step
    return [(y * 4 + x, (y + dy) % 2 * 4 + (x + dx) % 4) for y in range(2) for x in range(4)]


def on_device(inputs, cotangent, kernel, inner_weight, outer_weight, twiddle, up_weight, down_weight):
    mix_flops = 2 * BW * TOK * INNER
    col_flops = 4 * OUTER * OUTER * LANES
    mlp_flops = 2 * HB * BW * TOK
    send, first = call(
        rows_in,
        [((OUTER, LANES), bf16), ((BW, TOK), bf16)],
        inputs,
        inner_weight,
        twiddle,
        flops=mix_flops,
        scratch=[TURNED, STAGE],
    )

    cotangent_late, down_late, send = lax.optimization_barrier((cotangent, down_weight, send))
    block = jnp.concatenate([cotangent_late.astype(bf16), down_late], axis=1)
    shared = Stacked(gather_over_chan(block), (NBLK, BW, TOK + HB), block_places)

    kernel_t = kernel.astype(bf16).transpose(2, 1, 0).reshape(OUTER, LANES)
    outer_t = outer_weight.T
    up_t = up_weight.T

    recv = exchange(send)
    send, spectrum = call(
        columns,
        [((OUTER, LANES), bf16), ((OUTER, LANES), bf16)],
        recv,
        outer_weight,
        kernel_t,
        outer_t,
        flops=col_flops,
    )
    recv = exchange(send)
    send, later, direct = call(
        mlp,
        [((OUTER, WIDE), bf16), ((ROWS, INNER), f32), ((BW, TOK), f32)],
        recv,
        inner_weight,
        twiddle,
        inputs,
        up_weight,
        shared,
        up_t,
        cotangent,
        flops=2 * mix_flops + 5 * mlp_flops,
        trans=2 * HB * TOK,
        scratch=[
            TURNED,
            STAGE,
            TURNED,
            STAGE,
            pltpu.VMEM((HB, BW), f32),
            pltpu.VMEM((HB, BW), bf16),
            pltpu.VMEM((HB, BW), f32),
            pltpu.VMEM((HB, BW), f32),
        ],
    )
    recv = exchange(send)

    send, grad_spec = call(
        columns,
        [((OUTER, WIDE), bf16), ((OUTER, LANES), f32)],
        recv,
        outer_weight,
        kernel_t,
        outer_t,
        flops=col_flops,
    )
    recv = exchange(send)
    grad_kernel = (grad_spec * spectrum.astype(f32)).reshape(OUTER, COLS, BW).transpose(2, 1, 0)

    shared, grad_back, grad_up = call(
        twiddle_terms,
        [((NBLK, SLICE + 2 * ROWS, LANE_TILE), bf16), ((BW, TOK), bf16), ((HB, BW), f32)],
        recv,
        first,
        later,
        twiddle,
        scratch=[TURNED, STAGE],
    )
    shared = lax.all_to_all(shared, "chan", split_axis=0, concat_axis=0, tiled=True)
    (grad_inputs,) = call(
        rows_out, [((BW, TOK), f32)], grad_back, inner_weight, direct, flops=mix_flops
    )
    grad_down, grad_twiddle = call(finish, [((BW, HB), f32), ((ROWS, INNER), f32)], shared)
    return grad_inputs, grad_kernel, grad_up, grad_down, grad_twiddle


def solution(mesh):
    placed = (
        P("chan", "seq"),
        P("chan", "seq"),
        P("chan", "seq", None),
        P(),
        P(),
        P("seq", None),
        P("chan", None),
        P("chan", None),
    )
    return jax.shard_map(
        on_device,
        mesh=mesh,
        in_specs=placed,
        out_specs=(
            P("chan", "seq"),
            P("chan", "seq", None),
            P("chan", None),
            P("chan", None),
            P("seq", None),
        ),
        check_vma=False,
    )
```

```python
import functools
import math

import jax
import jax.numpy as jnp
from jax import lax
from jax.experimental import pallas as pl
from jax.experimental.pallas import tpu as pltpu
from jax.sharding import PartitionSpec as P

D = 768
HID = 3072
NBLK = 8
OUTER = 512
INNER = 256
SEQ = 131072
BW = D // NBLK
HB = HID // NBLK
SLICE = HB // NBLK
NSEQ = 64
ROWS = OUTER // NSEQ
COLS = INNER // NSEQ
LANES = COLS * BW
TOK = ROWS * INNER
LANE_TILE = 128
MIXED = ROWS // 2 * LANES
PIECES = 2 * HB // (2 * NSEQ)
WIDE = MIXED + (PIECES * BW + LANE_TILE - 1) // LANE_TILE * LANE_TILE

f32 = jnp.float32
bf16 = jnp.bfloat16
NT = (((1,), (1,)), ((), ()))
NN = (((1,), (0,)), ((), ()))


def dot(lhs, rhs, dims=NN):
    return lax.dot_general(lhs, rhs, dims, preferred_element_type=f32)


class Stacked:
    def __init__(self, parts, shape, places):
        self.parts, self.shape, self.places = parts, shape, places
        self.dtype = parts[0].dtype


def call(body, outs, *operands, flops=0, scratch=(), trans=0):
    shapes = [jax.ShapeDtypeStruct(shape, dtype) for shape, dtype in outs]
    nbytes = sum(math.prod(o.shape) * o.dtype.itemsize for o in list(operands) + shapes)
    arrays = []
    for operand in operands:
        arrays += list(operand.parts) if isinstance(operand, Stacked) else [operand]
    n_in, n_out = len(operands), len(shapes)

    def kernel(*refs):
        sources, targets, refs = refs[: len(arrays)], refs[len(arrays) : len(arrays) + n_out], refs[len(arrays) + n_out :]
        held, built, refs = refs[:n_in], refs[n_in : n_in + n_out], refs[n_in + n_out :]
        in_sems, out_sems, refs = refs[0], refs[1], refs[2:]
        loads, taken, n_copies = [], 0, 0
        for operand, ref in zip(operands, held):
            if isinstance(operand, Stacked):
                moves = [
                    (source.at[pl.ds(start, rows)], place)
                    for source, places in zip(sources[taken:], operand.places(ref))
                    for start, rows, place in places
                ]
                taken += len(operand.parts)
            else:
                moves = [(sources[taken], ref)]
                taken += 1
            copies = []
            for source, place in moves:
                copies.append(pltpu.make_async_copy(source, place, in_sems.at[n_copies]))
                copies[-1].start()
                n_copies += 1
            loads.append(copies)

        def ready(i):
            while loads[i]:
                loads[i].pop().wait()
            return held[i]

        stores = []

        class Out:
            def __init__(self, i):
                self.i, self.ref, self.parts = i, built[i], 0

            def store(self, *index):
                source = built[self.i].at[index] if index else built[self.i]
                target = targets[self.i].at[index] if index else targets[self.i]
                copy = pltpu.make_async_copy(source, target, out_sems.at[self.i, self.parts])
                self.parts += 1
                copy.start()
                stores.append(copy)

        out = [Out(i) for i in range(n_out)]
        body([functools.partial(ready, i) for i in range(n_in)], out, *refs)
        for i in range(n_in):
            ready(i)
        for o in out:
            if not o.parts:
                o.store()
        for copy in stores:
            copy.wait()

    return pl.pallas_call(
        kernel,
        out_shape=shapes,
        in_specs=[pl.BlockSpec(memory_space=pltpu.HBM)] * len(arrays),
        out_specs=[pl.BlockSpec(memory_space=pltpu.HBM)] * n_out,
        scratch_shapes=[pltpu.VMEM(o.shape, o.dtype) for o in list(operands) + shapes]
        + [pltpu.SemaphoreType.DMA((2 * len(arrays),)), pltpu.SemaphoreType.DMA((n_out, ROWS))]
        + list(scratch),
        cost_estimate=pl.CostEstimate(flops=flops, bytes_accessed=nbytes, transcendentals=trans),
        compiler_params=pltpu.CompilerParams(vmem_limit_bytes=60 * 1024 * 1024),
    )(*arrays)


def token_columns(a):
    return slice(a * INNER, (a + 1) * INNER)


def to_message(value, a, turned, stage):
    turned[:, :BW] = value.T
    parts = [turned[pl.ds(b, NSEQ, stride=COLS), :][:, :BW] for b in range(COLS)]
    row = jnp.concatenate(parts, axis=1)
    for k in range(LANES // LANE_TILE):
        stage[k, :, a, :] = row[:, k * LANE_TILE : (k + 1) * LANE_TILE]


def from_message(a, turned, stage):
    row = jnp.concatenate(
        [stage[k, :, a, :] for k in range(LANES // LANE_TILE)], axis=1
    )
    for b in range(COLS):
        turned[pl.ds(b, NSEQ, stride=COLS), :] = jnp.concatenate(
            [row[:, b * BW : (b + 1) * BW], jnp.zeros((NSEQ, LANE_TILE - BW), f32)], axis=1
        )
    return turned[...].T[:BW]


def lane_tile(k):
    return slice(k * LANE_TILE, (k + 1) * LANE_TILE)


def pack(stage, send_ref):
    for k in range(LANES // LANE_TILE):
        send_ref[:, lane_tile(k)] = stage[k].reshape(OUTER, LANE_TILE).astype(bf16)


def unpack(recv_ref, stage):
    for k in range(LANES // LANE_TILE):
        stage[k] = recv_ref[:, lane_tile(k)].astype(f32).reshape(NSEQ, ROWS, LANE_TILE)


def pairs():
    tiles = LANES // LANE_TILE
    return [(h * tiles + k, slice(2 * h, 2 * h + 2), k) for h in range(ROWS // 2) for k in range(tiles)]


def pack_wide(stage, send_ref):
    for tile, rows, k in pairs():
        send_ref[:, :, lane_tile(tile)] = stage[k, :, rows, :].astype(bf16)


def unpack_wide(recv_ref, stage):
    for tile, rows, k in pairs():
        stage[k, :, rows, :] = recv_ref[:, :, lane_tile(tile)].astype(f32)


STAGE = pltpu.VMEM((LANES // LANE_TILE, NSEQ, ROWS, LANE_TILE), f32)
TURNED = pltpu.VMEM((INNER, LANE_TILE), f32)


def rows_in(ins, outs, turned, stage):
    x, w, twiddle = ins
    send, first_out = outs
    for a in range(ROWS):
        cols = token_columns(a)
        first = dot(x()[:, cols].astype(bf16), w()[...], NT)
        first_out.ref[:, cols] = first.astype(bf16)
        to_message(first * twiddle()[a : a + 1, :], a, turned, stage)
    first_out.store()
    pack(stage, send.ref)


def columns(ins, outs):
    recv, outer, kernel, outer_t = ins
    send, spec_out = outs
    spec = dot(outer()[...], recv()[...])
    spec_out.ref[...] = spec.astype(bf16)
    spec_out.store()
    scaled = (kernel()[...].astype(f32) * spec).astype(bf16)
    send.ref[...] = dot(outer_t()[...], scaled).astype(bf16)


def columns_wide(ins, outs, stage):
    recv, outer, kernel, outer_t = ins
    send, spec_out = outs
    unpack_wide(recv(), stage)
    tiles = LANES // LANE_TILE
    rows = jnp.concatenate([stage[k].reshape(OUTER, LANE_TILE).astype(bf16) for k in range(tiles)], axis=1)
    spec = dot(outer()[...], rows)
    spec_out.ref[...] = spec
    spec_out.store()
    total = jnp.sum(recv()[:, :, MIXED:].astype(f32), axis=0, keepdims=True)
    send.ref[:, :, MIXED:] = jnp.broadcast_to(total, (NSEQ, 2, WIDE - MIXED)).astype(bf16)
    scaled = (kernel()[...].astype(f32) * spec).astype(bf16)
    back = dot(outer_t()[...], scaled)
    for k in range(tiles):
        stage[k] = back[:, lane_tile(k)].reshape(NSEQ, ROWS, LANE_TILE)
    pack_wide(stage, send.ref)


def mlp(ins, outs, turned, stage, turned_out, stage_out, down_t, down_own, grad_up, grad_down):
    recv, w, twiddle, x_in, up, shared, up_t, cot = ins
    send, later, direct = outs
    me = lax.axis_index("chan")
    unpack(recv(), stage)
    for a in range(ROWS):
        cols = token_columns(a)
        scale = twiddle()[a : a + 1, :]
        back = from_message(a, turned, stage)
        mixing = dot((back * scale).astype(bf16), w()[...])
        x = x_in()[:, cols]
        low = (x + x * mixing).astype(bf16)
        hidden = dot(up()[...], low)
        cumulative = 0.5 * (1.0 + lax.erf(hidden * (1.0 / math.sqrt(2.0))))
        density = jnp.exp(-0.5 * hidden * hidden) * (1.0 / math.sqrt(2.0 * math.pi))
        act = (hidden * cumulative).astype(bf16)
        slope = cumulative + hidden * density
        if a == 0:
            for p in range(NBLK):
                down_t[...] = shared()[p, :, TOK:].astype(f32).T
                own = pl.ds(pl.multiple_of(me * SLICE, SLICE), SLICE)
                down_own[p * SLICE : (p + 1) * SLICE, :] = down_t[own, :].astype(bf16)
        grad_act, down_part = [], []
        for p in range(NBLK):
            rows = slice(p * SLICE, (p + 1) * SLICE)
            cot_low = shared()[p, :, cols]
            grad_act.append(dot(down_own[rows, :], cot_low).astype(bf16))
            down_part.append(dot(act[rows], cot_low, NT))
        grad_act = jnp.concatenate(grad_act, axis=0).astype(f32)
        down_part = jnp.concatenate(down_part, axis=0)
        grad_hidden = (grad_act * slope).astype(bf16)
        up_part = dot(grad_hidden, low, NT)
        if a == 0:
            grad_up[...] = up_part
            grad_down[...] = down_part
        else:
            grad_up[...] += up_part
            grad_down[...] += down_part
        grad_gated = cot()[:, cols] + dot(up_t()[...], grad_hidden)
        direct.ref[:, cols] = grad_gated * (1.0 + mixing)
        direct.store(slice(None), cols)
        grad_mix = (grad_gated * x).astype(bf16)
        second = dot(grad_mix, w()[...], NT)
        later.ref[a : a + 1, :] = jnp.sum(second * back, axis=0, keepdims=True)
        to_message(second * scale, a, turned_out, stage_out)
    pack_wide(stage_out, send.ref)
    grads = jnp.concatenate([grad_up[...], grad_down[...]], axis=0)
    pieces = [grads[i * 2 * NSEQ : (i + 1) * 2 * NSEQ] for i in range(PIECES)]
    pieces.append(jnp.zeros((2 * NSEQ, WIDE - MIXED - PIECES * BW), f32))
    grads = jnp.concatenate(pieces, axis=1).reshape(NSEQ, 2, WIDE - MIXED)
    send.ref[:, :, MIXED:] = grads.astype(bf16)


def gather_over_chan(block):
    straight = [lax.ppermute(block, "chan", step_to(step)) for step in ((1, 0), (0, 1), (0, 3), (1, 2))]
    across, left, right, far = lax.optimization_barrier(straight)
    half = BW // 2
    onward_left = lax.ppermute(jnp.concatenate([across, left[:half]]), "chan", step_to((0, 1)))
    onward_right = lax.ppermute(jnp.concatenate([across, right[half:]]), "chan", step_to((0, 3)))
    return block, across, left, right, far, onward_left, onward_right


def block_places(ref):
    me = lax.axis_index("chan")
    half = BW // 2

    def at(dy, dx):
        return ref.at[(me // 4 + dy) % 2 * 4 + (me % 4 + dx) % 4]

    return [
        [(0, BW, at(0, 0))],
        [(0, BW, at(1, 0))],
        [(0, BW, at(0, 3))],
        [(0, BW, at(0, 1))],
        [(0, BW, at(1, 2))],
        [(0, BW, at(1, 3)), (BW, half, at(0, 2).at[pl.ds(0, half)])],
        [(0, BW, at(1, 1)), (BW, half, at(0, 2).at[pl.ds(half, half)])],
    ]


def twiddle_terms(ins, outs, turned, stage):
    recv, first, later, twiddle = ins
    shared, grad_back_out, grad_up = outs
    unpack_wide(recv(), stage)
    terms = []
    for a in range(ROWS):
        cols = token_columns(a)
        grad_back = from_message(a, turned, stage)
        terms.append(
            jnp.sum(grad_back * first()[:, cols].astype(f32), axis=0, keepdims=True) + later()[a : a + 1, :]
        )
        grad_back_out.ref[:, cols] = (grad_back * twiddle()[a : a + 1, :]).astype(bf16)
    grad_back_out.store()
    terms = jnp.concatenate(terms, axis=0)
    terms = jnp.concatenate([terms[:, :LANE_TILE], terms[:, LANE_TILE:]], axis=0).astype(bf16)
    grads = recv()[:, :, MIXED:].astype(f32).reshape(2 * NSEQ, WIDE - MIXED)
    grads = jnp.concatenate([grads[:, i * BW : (i + 1) * BW] for i in range(PIECES)], axis=0)
    grad_up.ref[...] = grads[:HB] * (1.0 / math.sqrt(SEQ))
    zeros = jnp.zeros((SLICE, LANE_TILE - BW), f32)
    for p in range(NBLK):
        rows = slice(HB + p * SLICE, HB + (p + 1) * SLICE)
        shared.ref[p, :SLICE, :] = jnp.concatenate([grads[rows], zeros], axis=1).astype(bf16)
        shared.ref[p, SLICE:, :] = terms


def rows_out(ins, outs):
    grad_back, w, direct = ins
    (out,) = outs
    for a in range(ROWS):
        cols = token_columns(a)
        out.ref[:, cols] = direct()[:, cols] + dot(grad_back()[:, cols], w()[...])
        out.store(slice(None), cols)


def finish(ins, outs):
    (shared,) = ins
    grad_down, grad_twiddle = outs
    terms = jnp.sum(shared()[:, SLICE:, :].astype(f32), axis=0) * (1.0 / math.sqrt(D))
    grad_twiddle.ref[:, :LANE_TILE] = terms[:ROWS]
    grad_twiddle.ref[:, LANE_TILE:] = terms[ROWS:]
    down = jnp.concatenate([shared()[j, :SLICE, :].astype(f32) for j in range(NBLK)], axis=0)
    grad_down.ref[...] = down.T[:BW] * (1.0 / math.sqrt(SEQ))


def exchange(values):
    return lax.all_to_all(
        values.reshape(NSEQ, -1, values.shape[-1]), "seq", split_axis=0, concat_axis=0, tiled=True
    ).reshape(values.shape)


def step_to(step):
    dy, dx = step
    return [(y * 4 + x, (y + dy) % 2 * 4 + (x + dx) % 4) for y in range(2) for x in range(4)]


def on_device(inputs, cotangent, kernel, inner_weight, outer_weight, twiddle, up_weight, down_weight):
    mix_flops = 2 * BW * TOK * INNER
    col_flops = 4 * OUTER * OUTER * LANES
    mlp_flops = 2 * HB * BW * TOK
    send, first = call(
        rows_in,
        [((OUTER, LANES), bf16), ((BW, TOK), bf16)],
        inputs,
        inner_weight,
        twiddle,
        flops=mix_flops,
        scratch=[TURNED, STAGE],
    )

    cotangent_late, down_late, send = lax.optimization_barrier((cotangent, down_weight, send))
    block = jnp.concatenate([cotangent_late.astype(bf16), down_late], axis=1)
    shared = Stacked(gather_over_chan(block), (NBLK, BW, TOK + HB), block_places)

    kernel_t = kernel.astype(bf16).transpose(2, 1, 0).reshape(OUTER, LANES)
    outer_t = outer_weight.T
    up_t = up_weight.T

    recv = exchange(send)
    send, spectrum = call(
        columns,
        [((OUTER, LANES), bf16), ((OUTER, LANES), bf16)],
        recv,
        outer_weight,
        kernel_t,
        outer_t,
        flops=col_flops,
    )
    recv = exchange(send)
    send, later, direct = call(
        mlp,
        [((NSEQ, 2, WIDE), bf16), ((ROWS, INNER), f32), ((BW, TOK), f32)],
        recv,
        inner_weight,
        twiddle,
        inputs,
        up_weight,
        shared,
        up_t,
        cotangent,
        flops=2 * mix_flops + 5 * mlp_flops,
        trans=2 * HB * TOK,
        scratch=[
            TURNED,
            STAGE,
            TURNED,
            STAGE,
            pltpu.VMEM((HB, BW), f32),
            pltpu.VMEM((HB, BW), bf16),
            pltpu.VMEM((HB, BW), f32),
            pltpu.VMEM((HB, BW), f32),
        ],
    )
    recv = exchange(send)

    send, grad_spec = call(
        columns_wide,
        [((NSEQ, 2, WIDE), bf16), ((OUTER, LANES), f32)],
        recv,
        outer_weight,
        kernel_t,
        outer_t,
        flops=col_flops,
        scratch=[STAGE],
    )
    recv = exchange(send)
    grad_kernel = (grad_spec * spectrum.astype(f32)).reshape(OUTER, COLS, BW).transpose(2, 1, 0)

    shared, grad_back, grad_up = call(
        twiddle_terms,
        [((NBLK, SLICE + 2 * ROWS, LANE_TILE), bf16), ((BW, TOK), bf16), ((HB, BW), f32)],
        recv,
        first,
        later,
        twiddle,
        scratch=[TURNED, STAGE],
    )
    shared = lax.all_to_all(shared, "chan", split_axis=0, concat_axis=0, tiled=True)
    (grad_inputs,) = call(
        rows_out, [((BW, TOK), f32)], grad_back, inner_weight, direct, flops=mix_flops
    )
    grad_down, grad_twiddle = call(finish, [((BW, HB), f32), ((ROWS, INNER), f32)], shared)
    return grad_inputs, grad_kernel, grad_up, grad_down, grad_twiddle


def solution(mesh):
    placed = (
        P("chan", "seq"),
        P("chan", "seq"),
        P("chan", "seq", None),
        P(),
        P(),
        P("seq", None),
        P("chan", None),
        P("chan", None),
    )
    return jax.shard_map(
        on_device,
        mesh=mesh,
        in_specs=placed,
        out_specs=(
            P("chan", "seq"),
            P("chan", "seq", None),
            P("chan", None),
            P("chan", None),
            P("seq", None),
        ),
        check_vma=False,
    )
```

```python
import functools
import math

import jax
import jax.numpy as jnp
from jax import lax
from jax.experimental import pallas as pl
from jax.experimental.pallas import tpu as pltpu
from jax.sharding import PartitionSpec as P

D = 768
HID = 3072
NBLK = 8
OUTER = 512
INNER = 256
SEQ = 131072
BW = D // NBLK
HB = HID // NBLK
SLICE = HB // NBLK
NSEQ = 64
ROWS = OUTER // NSEQ
COLS = INNER // NSEQ
LANES = COLS * BW
TOK = ROWS * INNER
LANE_TILE = 128
MIXED = ROWS // 2 * LANES
PIECES = 2 * HB // (2 * NSEQ)
WIDE = MIXED + (PIECES * BW + LANE_TILE - 1) // LANE_TILE * LANE_TILE

f32 = jnp.float32
bf16 = jnp.bfloat16
HIDE_FLOPS = 14 * 10**9
NT = (((1,), (1,)), ((), ()))
NN = (((1,), (0,)), ((), ()))


def dot(lhs, rhs, dims=NN):
    return lax.dot_general(lhs, rhs, dims, preferred_element_type=f32)


class Stacked:
    def __init__(self, parts, shape, places):
        self.parts, self.shape, self.places = parts, shape, places
        self.dtype = parts[0].dtype


def call(body, outs, *operands, flops=0, scratch=(), trans=0, arrived=(0,), grant=32):
    shapes = [jax.ShapeDtypeStruct(shape, dtype) for shape, dtype in outs]
    nbytes = sum(math.prod(o.shape) * o.dtype.itemsize for o in list(operands) + shapes)
    arrays, specs = [], []
    for i, operand in enumerate(operands):
        parts = list(operand.parts) if isinstance(operand, Stacked) else [operand]
        arrays += parts
        specs += [pl.BlockSpec(memory_space=pl.ANY if i in arrived else pltpu.HBM)] * len(parts)
    n_in, n_out = len(operands), len(shapes)

    def kernel(*refs):
        sources, targets, refs = refs[: len(arrays)], refs[len(arrays) : len(arrays) + n_out], refs[len(arrays) + n_out :]
        held, built, refs = refs[:n_in], refs[n_in : n_in + n_out], refs[n_in + n_out :]
        in_sems, out_sems, refs = refs[0], refs[1], refs[2:]
        loads, taken = [], 0
        for operand, ref in zip(operands, held):
            if isinstance(operand, Stacked):
                places = operand.places(ref)
            else:
                places = [ref]
            copies = []
            for place in places:
                copies.append(pltpu.make_async_copy(sources[taken], place, in_sems.at[taken]))
                copies[-1].start()
                taken += 1
            loads.append(copies)

        def ready(i):
            while loads[i]:
                loads[i].pop().wait()
            return held[i]

        stores = []

        class Out:
            def __init__(self, i):
                self.i, self.ref, self.parts = i, built[i], 0

            def store(self, *index):
                source = built[self.i].at[index] if index else built[self.i]
                target = targets[self.i].at[index] if index else targets[self.i]
                copy = pltpu.make_async_copy(source, target, out_sems.at[self.i, self.parts])
                self.parts += 1
                copy.start()
                stores.append(copy)

        out = [Out(i) for i in range(n_out)]
        body([functools.partial(ready, i) for i in range(n_in)], out, *refs)
        for i in range(n_in):
            ready(i)
        for o in out:
            if not o.parts:
                o.store()
        for copy in stores:
            copy.wait()

    return pl.pallas_call(
        kernel,
        out_shape=shapes,
        in_specs=specs,
        out_specs=[pl.BlockSpec(memory_space=pltpu.HBM)] * n_out,
        scratch_shapes=[pltpu.VMEM(o.shape, o.dtype) for o in list(operands) + shapes]
        + [pltpu.SemaphoreType.DMA((len(arrays),)), pltpu.SemaphoreType.DMA((n_out, ROWS))]
        + list(scratch),
        cost_estimate=pl.CostEstimate(flops=flops, bytes_accessed=nbytes, transcendentals=trans),
        compiler_params=pltpu.CompilerParams(vmem_limit_bytes=grant * 1024 * 1024),
    )(*arrays)


def token_columns(a):
    return slice(a * INNER, (a + 1) * INNER)


def to_message(value, a, turned, stage):
    turned[:, :BW] = value.T
    parts = [turned[pl.ds(b, NSEQ, stride=COLS), :][:, :BW] for b in range(COLS)]
    row = jnp.concatenate(parts, axis=1)
    for k in range(LANES // LANE_TILE):
        stage[k, :, a, :] = row[:, k * LANE_TILE : (k + 1) * LANE_TILE]


def from_message(a, turned, stage):
    row = jnp.concatenate(
        [stage[k, :, a, :] for k in range(LANES // LANE_TILE)], axis=1
    )
    for b in range(COLS):
        turned[pl.ds(b, NSEQ, stride=COLS), :] = jnp.concatenate(
            [row[:, b * BW : (b + 1) * BW], jnp.zeros((NSEQ, LANE_TILE - BW), f32)], axis=1
        )
    return turned[...].T[:BW]


def lane_tile(k):
    return slice(k * LANE_TILE, (k + 1) * LANE_TILE)


def pack(stage, send_ref):
    for k in range(LANES // LANE_TILE):
        send_ref[:, lane_tile(k)] = stage[k].reshape(OUTER, LANE_TILE).astype(bf16)


def unpack(recv_ref, stage):
    for k in range(LANES // LANE_TILE):
        stage[k] = recv_ref[:, lane_tile(k)].astype(f32).reshape(NSEQ, ROWS, LANE_TILE)


def pairs():
    tiles = LANES // LANE_TILE
    return [(h * tiles + k, slice(2 * h, 2 * h + 2), k) for h in range(ROWS // 2) for k in range(tiles)]


def pack_wide(stage, send_ref):
    for tile, rows, k in pairs():
        send_ref[:, :, lane_tile(tile)] = stage[k, :, rows, :].astype(bf16)


def unpack_wide(recv_ref, stage):
    for tile, rows, k in pairs():
        stage[k, :, rows, :] = recv_ref[:, :, lane_tile(tile)].astype(f32)


STAGE = pltpu.VMEM((LANES // LANE_TILE, NSEQ, ROWS, LANE_TILE), f32)
TURNED = pltpu.VMEM((INNER, LANE_TILE), f32)


def rows_in(ins, outs, turned, stage):
    x, w, twiddle = ins
    send, first_out = outs
    for a in range(ROWS):
        cols = token_columns(a)
        first = dot(x()[:, cols].astype(bf16), w()[...], NT)
        first_out.ref[:, cols] = first.astype(bf16)
        to_message(first * twiddle()[a : a + 1, :], a, turned, stage)
    first_out.store()
    pack(stage, send.ref)


def transpose_up(ins, outs):
    (up,) = ins
    outs[0].ref[...] = up()[...].astype(f32).T.astype(bf16)


def prepare(ins, outs):
    outer, kernel = ins
    outer_t, kernel_t = outs
    outer_t.ref[...] = outer()[...].astype(f32).T.astype(bf16)
    parts = [kernel()[:, b, :].T for b in range(COLS)]
    kernel_t.ref[...] = jnp.concatenate(parts, axis=1).astype(bf16)


def columns(ins, outs):
    recv, outer, kernel, outer_t = ins
    send, spec_out = outs
    spec = dot(outer()[...], recv()[...])
    spec_out.ref[...] = spec.astype(bf16)
    spec_out.store()
    scaled = (kernel()[...].astype(f32) * spec).astype(bf16)
    send.ref[...] = dot(outer_t()[...], scaled).astype(bf16)


def columns_wide(ins, outs, stage):
    recv, outer, kernel, outer_t = ins
    send, spec_out = outs
    unpack_wide(recv(), stage)
    tiles = LANES // LANE_TILE
    rows = jnp.concatenate([stage[k].reshape(OUTER, LANE_TILE).astype(bf16) for k in range(tiles)], axis=1)
    spec = dot(outer()[...], rows)
    spec_out.ref[...] = spec
    spec_out.store()
    total = jnp.sum(recv()[:, :, MIXED:].astype(f32), axis=0, keepdims=True)
    send.ref[:, :, MIXED:] = jnp.broadcast_to(total, (NSEQ, 2, WIDE - MIXED)).astype(bf16)
    scaled = (kernel()[...].astype(f32) * spec).astype(bf16)
    back = dot(outer_t()[...], scaled)
    for k in range(tiles):
        stage[k] = back[:, lane_tile(k)].reshape(NSEQ, ROWS, LANE_TILE)
    pack_wide(stage, send.ref)


def mlp(ins, outs, turned, stage, turned_out, stage_out, down_own, grad_up, grad_down):
    recv, w, twiddle, x_in, up, shared, up_t, cot = ins
    send, later, direct = outs
    me = lax.axis_index("chan")
    unpack(recv(), stage)
    for a in range(ROWS):
        cols = token_columns(a)
        scale = twiddle()[a : a + 1, :]
        back = from_message(a, turned, stage)
        mixing = dot((back * scale).astype(bf16), w()[...])
        x = x_in()[:, cols]
        low = (x + x * mixing).astype(bf16)
        hidden = dot(up()[...], low)
        cumulative = 0.5 * (1.0 + lax.erf(hidden * (1.0 / math.sqrt(2.0))))
        density = jnp.exp(-0.5 * hidden * hidden) * (1.0 / math.sqrt(2.0 * math.pi))
        act = (hidden * cumulative).astype(bf16)
        slope = cumulative + hidden * density
        if a == 0:
            column = lax.broadcasted_iota(jnp.int32, (SLICE, HB), 1)
            own = column == lax.broadcasted_iota(jnp.int32, (SLICE, HB), 0) + me * SLICE
            own = jnp.where(own, 1.0, 0.0).astype(bf16)
            for p in range(NBLK):
                down_own[p * SLICE : (p + 1) * SLICE, :] = dot(own, shared()[p, :, TOK:], NT).astype(bf16)
        grad_act = []
        for p in range(NBLK):
            rows = slice(p * SLICE, (p + 1) * SLICE)
            grad_act.append(dot(down_own[rows, :], shared()[p, :, cols]).astype(bf16))
        grad_act = jnp.concatenate(grad_act, axis=0).astype(f32)
        down_part = [
            dot(act[2 * p * SLICE : 2 * (p + 1) * SLICE], shared()[2 * p : 2 * p + 2, :, cols].reshape(2 * BW, INNER), NT)
            for p in range(NBLK // 2)
        ]
        down_part = jnp.concatenate(down_part, axis=0)
        grad_hidden = (grad_act * slope).astype(bf16)
        up_part = dot(grad_hidden, low, NT)
        if a == 0:
            grad_up[...] = up_part
            grad_down[...] = down_part
        else:
            grad_up[...] += up_part
            grad_down[...] += down_part
        grad_gated = cot()[:, cols] + dot(up_t()[...], grad_hidden)
        direct.ref[:, cols] = grad_gated * (1.0 + mixing)
        direct.store(slice(None), cols)
        grad_mix = (grad_gated * x).astype(bf16)
        second = dot(grad_mix, w()[...], NT)
        later.ref[a : a + 1, :] = jnp.sum(second * back, axis=0, keepdims=True)
        to_message(second * scale, a, turned_out, stage_out)
    pack_wide(stage_out, send.ref)
    grads = [grad_up[...]]
    for p in range(NBLK):
        grads.append(grad_down[p * SLICE : (p + 1) * SLICE, p % 2 * BW : (p % 2 + 1) * BW])
    grads = jnp.concatenate(grads, axis=0)
    pieces = [grads[i * 2 * NSEQ : (i + 1) * 2 * NSEQ] for i in range(PIECES)]
    pieces.append(jnp.zeros((2 * NSEQ, WIDE - MIXED - PIECES * BW), f32))
    grads = jnp.concatenate(pieces, axis=1).reshape(NSEQ, 2, WIDE - MIXED)
    send.ref[:, :, MIXED:] = grads.astype(bf16)


def gather_over_chan(block):
    steps = ((1, 0), (0, 1), (0, 3), (1, 2))
    straight = lax.optimization_barrier([lax.ppermute(block, "chan", step_to(step)) for step in steps])
    across, far = straight[0], straight[3]
    onward = [
        lax.ppermute(values, "chan", step_to(step)) for values, step in ((far, (1, 0)), (across, (0, 1)), (across, (0, 3)))
    ]
    return [block, *straight, *onward]


def block_places(ref):
    me = lax.axis_index("chan")
    steps = ((0, 0), (1, 0), (0, 3), (0, 1), (1, 2), (0, 2), (1, 3), (1, 1))
    return [ref.at[(me // 4 + dy) % 2 * 4 + (me % 4 + dx) % 4] for dy, dx in steps]


def twiddle_terms(ins, outs, turned, stage):
    recv, first, later = ins
    (shared,) = outs
    unpack_wide(recv(), stage)
    terms = []
    for a in range(ROWS):
        grad_back = from_message(a, turned, stage)
        early = jnp.sum(grad_back * first()[:, token_columns(a)].astype(f32), axis=0, keepdims=True)
        terms.append(early + later()[a : a + 1, :])
    terms = jnp.concatenate(terms, axis=0)
    terms = jnp.concatenate([terms[:, :LANE_TILE], terms[:, LANE_TILE:]], axis=0).astype(bf16)
    grads = weight_grads(recv())[HB:]
    zeros = jnp.zeros((SLICE, LANE_TILE - BW), f32)
    for p in range(NBLK):
        rows = slice(p * SLICE, (p + 1) * SLICE)
        shared.ref[p, :SLICE, :] = jnp.concatenate([grads[rows], zeros], axis=1).astype(bf16)
        shared.ref[p, SLICE:, :] = terms


def weight_grads(recv_ref):
    grads = recv_ref[:, :, MIXED:].astype(f32).reshape(2 * NSEQ, WIDE - MIXED)
    return jnp.concatenate([grads[:, i * BW : (i + 1) * BW] for i in range(PIECES)], axis=0)


def rows_out(ins, outs, turned, stage):
    recv, twiddle, w, direct = ins
    out, grad_up = outs
    unpack_wide(recv(), stage)
    for a in range(ROWS):
        cols = token_columns(a)
        grad_back = from_message(a, turned, stage)
        out.ref[:, cols] = direct()[:, cols] + dot((grad_back * twiddle()[a : a + 1, :]).astype(bf16), w()[...])
        out.store(slice(None), cols)
    grad_up.ref[...] = weight_grads(recv())[:HB] * (1.0 / math.sqrt(SEQ))


def finish(ins, outs):
    (shared,) = ins
    grad_down, grad_twiddle = outs
    terms = jnp.sum(shared()[:, SLICE:, :].astype(f32), axis=0) * (1.0 / math.sqrt(D))
    grad_twiddle.ref[:, :LANE_TILE] = terms[:ROWS]
    grad_twiddle.ref[:, LANE_TILE:] = terms[ROWS:]
    down = jnp.concatenate([shared()[j, :SLICE, :].astype(f32) for j in range(NBLK)], axis=0)
    grad_down.ref[...] = down.T[:BW] * (1.0 / math.sqrt(SEQ))


def exchange(values):
    return lax.all_to_all(
        values.reshape(NSEQ, -1, values.shape[-1]), "seq", split_axis=0, concat_axis=0, tiled=True
    ).reshape(values.shape)


def step_to(step):
    dy, dx = step
    return [(y * 4 + x, (y + dy) % 2 * 4 + (x + dx) % 4) for y in range(2) for x in range(4)]


def on_device(inputs, cotangent, kernel, inner_weight, outer_weight, twiddle, up_weight, down_weight):
    mix_flops = 2 * BW * TOK * INNER
    col_flops = 4 * OUTER * OUTER * LANES
    mlp_flops = 2 * HB * BW * TOK
    send, first = call(
        rows_in,
        [((OUTER, LANES), bf16), ((BW, TOK), bf16)],
        inputs,
        inner_weight,
        twiddle,
        flops=mix_flops,
        scratch=[TURNED, STAGE],
        arrived=(),
        grant=60,
    )

    cotangent_late, down_late, send = lax.optimization_barrier((cotangent, down_weight, send))
    block = jnp.concatenate([cotangent_late.astype(bf16), down_late], axis=1)
    shared = Stacked(gather_over_chan(block), (NBLK, BW, TOK + HB), block_places)

    kernel_late, send = lax.optimization_barrier((kernel, send))
    outer_t, kernel_t = call(
        prepare, [((OUTER, OUTER), bf16), ((OUTER, LANES), bf16)], outer_weight, kernel_late, arrived=()
    )
    (up_t,) = call(transpose_up, [((BW, HB), bf16)], up_weight, flops=HIDE_FLOPS, arrived=())

    recv = exchange(send)
    send, spectrum = call(
        columns,
        [((OUTER, LANES), bf16), ((OUTER, LANES), bf16)],
        recv,
        outer_weight,
        kernel_t,
        outer_t,
        flops=col_flops,
    )
    recv = exchange(send)
    send, later, direct = call(
        mlp,
        [((NSEQ, 2, WIDE), bf16), ((ROWS, INNER), f32), ((BW, TOK), f32)],
        recv,
        inner_weight,
        twiddle,
        inputs,
        up_weight,
        shared,
        up_t,
        cotangent,
        arrived=(0, 5),
        grant=60,
        flops=2 * mix_flops + 5 * mlp_flops,
        trans=2 * HB * TOK,
        scratch=[
            TURNED,
            STAGE,
            TURNED,
            STAGE,
            pltpu.VMEM((HB, BW), bf16),
            pltpu.VMEM((HB, BW), f32),
            pltpu.VMEM((HB, 2 * BW), f32),
        ],
    )
    recv = exchange(send)

    send, grad_spec = call(
        columns_wide,
        [((NSEQ, 2, WIDE), bf16), ((OUTER, LANES), f32)],
        recv,
        outer_weight,
        kernel_t,
        outer_t,
        flops=col_flops,
        scratch=[STAGE],
    )
    recv = exchange(send)
    grad_kernel = (grad_spec * spectrum.astype(f32)).reshape(OUTER, COLS, BW).transpose(2, 1, 0)

    (shared,) = call(
        twiddle_terms,
        [((NBLK, SLICE + 2 * ROWS, LANE_TILE), bf16)],
        recv,
        first,
        later,
        scratch=[TURNED, STAGE],
    )
    shared = lax.all_to_all(shared, "chan", split_axis=0, concat_axis=0, tiled=True)
    grad_inputs, grad_up = call(
        rows_out,
        [((BW, TOK), f32), ((HB, BW), f32)],
        recv,
        twiddle,
        inner_weight,
        direct,
        flops=mix_flops,
        scratch=[TURNED, STAGE],
    )
    grad_down, grad_twiddle = call(finish, [((BW, HB), f32), ((ROWS, INNER), f32)], shared)
    return grad_inputs, grad_kernel, grad_up, grad_down, grad_twiddle


def solution(mesh):
    placed = (
        P("chan", "seq"),
        P("chan", "seq"),
        P("chan", "seq", None),
        P(),
        P(),
        P("seq", None),
        P("chan", None),
        P("chan", None),
    )
    return jax.shard_map(
        on_device,
        mesh=mesh,
        in_specs=placed,
        out_specs=(
            P("chan", "seq"),
            P("chan", "seq", None),
            P("chan", None),
            P("chan", None),
            P("seq", None),
        ),
        check_vma=False,
    )
```

```python
import functools
import math

import jax
import jax.numpy as jnp
from jax import lax
from jax.experimental import pallas as pl
from jax.experimental.pallas import tpu as pltpu
from jax.sharding import PartitionSpec as P

D = 768
HID = 3072
NBLK = 8
OUTER = 512
INNER = 256
SEQ = 131072
BW = D // NBLK
HB = HID // NBLK
SLICE = HB // NBLK
NSEQ = 64
ROWS = OUTER // NSEQ
COLS = INNER // NSEQ
LANES = COLS * BW
TOK = ROWS * INNER
LANE_TILE = 128
MIXED = ROWS // 2 * LANES
PIECES = 2 * HB // (2 * NSEQ)
WIDE = MIXED + (PIECES * BW + LANE_TILE - 1) // LANE_TILE * LANE_TILE

f32 = jnp.float32
bf16 = jnp.bfloat16
HIDE_FLOPS = 14 * 10**9
NT = (((1,), (1,)), ((), ()))
NN = (((1,), (0,)), ((), ()))


def dot(lhs, rhs, dims=NN):
    return lax.dot_general(lhs, rhs, dims, preferred_element_type=f32)


class Stacked:
    def __init__(self, parts, shape, places):
        self.parts, self.shape, self.places = parts, shape, places
        self.dtype = parts[0].dtype


def call(body, outs, *operands, flops=0, scratch=(), trans=0, arrived=(0,), grant=32):
    shapes = [jax.ShapeDtypeStruct(shape, dtype) for shape, dtype in outs]
    nbytes = sum(math.prod(o.shape) * o.dtype.itemsize for o in list(operands) + shapes)
    arrays, specs = [], []
    for i, operand in enumerate(operands):
        parts = list(operand.parts) if isinstance(operand, Stacked) else [operand]
        arrays += parts
        specs += [pl.BlockSpec(memory_space=pl.ANY if i in arrived else pltpu.HBM)] * len(parts)
    n_in, n_out = len(operands), len(shapes)

    def kernel(*refs):
        sources, targets, refs = refs[: len(arrays)], refs[len(arrays) : len(arrays) + n_out], refs[len(arrays) + n_out :]
        held, built, refs = refs[:n_in], refs[n_in : n_in + n_out], refs[n_in + n_out :]
        in_sems, out_sems, refs = refs[0], refs[1], refs[2:]
        loads, taken = [], 0
        for operand, ref in zip(operands, held):
            if isinstance(operand, Stacked):
                places = operand.places(ref)
            else:
                places = [ref]
            copies = []
            for place in places:
                copies.append(pltpu.make_async_copy(sources[taken], place, in_sems.at[taken]))
                copies[-1].start()
                taken += 1
            loads.append(copies)

        def ready(i):
            while loads[i]:
                loads[i].pop().wait()
            return held[i]

        stores = []

        class Out:
            def __init__(self, i):
                self.i, self.ref, self.parts = i, built[i], 0

            def store(self, *index):
                source = built[self.i].at[index] if index else built[self.i]
                target = targets[self.i].at[index] if index else targets[self.i]
                copy = pltpu.make_async_copy(source, target, out_sems.at[self.i, self.parts])
                self.parts += 1
                copy.start()
                stores.append(copy)

        out = [Out(i) for i in range(n_out)]
        body([functools.partial(ready, i) for i in range(n_in)], out, *refs)
        for i in range(n_in):
            ready(i)
        for o in out:
            if not o.parts:
                o.store()
        for copy in stores:
            copy.wait()

    return pl.pallas_call(
        kernel,
        out_shape=shapes,
        in_specs=specs,
        out_specs=[pl.BlockSpec(memory_space=pltpu.HBM)] * n_out,
        scratch_shapes=[pltpu.VMEM(o.shape, o.dtype) for o in list(operands) + shapes]
        + [pltpu.SemaphoreType.DMA((len(arrays),)), pltpu.SemaphoreType.DMA((n_out, ROWS))]
        + list(scratch),
        cost_estimate=pl.CostEstimate(flops=flops, bytes_accessed=nbytes, transcendentals=trans),
        compiler_params=pltpu.CompilerParams(vmem_limit_bytes=grant * 1024 * 1024),
    )(*arrays)


def token_columns(a):
    return slice(a * INNER, (a + 1) * INNER)


def to_message(value, a, turned, stage):
    turned[:, :BW] = value.T
    parts = [turned[pl.ds(b, NSEQ, stride=COLS), :][:, :BW] for b in range(COLS)]
    row = jnp.concatenate(parts, axis=1)
    for k in range(LANES // LANE_TILE):
        stage[k, :, a, :] = row[:, k * LANE_TILE : (k + 1) * LANE_TILE]


def from_message(a, turned, stage):
    row = jnp.concatenate(
        [stage[k, :, a, :] for k in range(LANES // LANE_TILE)], axis=1
    )
    for b in range(COLS):
        turned[pl.ds(b, NSEQ, stride=COLS), :] = jnp.concatenate(
            [row[:, b * BW : (b + 1) * BW], jnp.zeros((NSEQ, LANE_TILE - BW), f32)], axis=1
        )
    return turned[...].T[:BW]


def lane_tile(k):
    return slice(k * LANE_TILE, (k + 1) * LANE_TILE)


def pack(stage, send_ref):
    for k in range(LANES // LANE_TILE):
        send_ref[:, lane_tile(k)] = stage[k].reshape(OUTER, LANE_TILE).astype(bf16)


def unpack(recv_ref, stage):
    for k in range(LANES // LANE_TILE):
        stage[k] = recv_ref[:, lane_tile(k)].astype(f32).reshape(NSEQ, ROWS, LANE_TILE)


def pairs():
    tiles = LANES // LANE_TILE
    return [(h * tiles + k, slice(2 * h, 2 * h + 2), k) for h in range(ROWS // 2) for k in range(tiles)]


def pack_wide(stage, send_ref):
    for tile, rows, k in pairs():
        send_ref[:, :, lane_tile(tile)] = stage[k, :, rows, :].astype(bf16)


def unpack_wide(recv_ref, stage):
    for tile, rows, k in pairs():
        stage[k, :, rows, :] = recv_ref[:, :, lane_tile(tile)].astype(f32)


STAGE = pltpu.VMEM((LANES // LANE_TILE, NSEQ, ROWS, LANE_TILE), f32)
TURNED = pltpu.VMEM((INNER, LANE_TILE), f32)


def rows_in(ins, outs, turned, stage):
    x, w, twiddle = ins
    send, first_out = outs
    for a in range(ROWS):
        cols = token_columns(a)
        first = dot(x()[:, cols].astype(bf16), w()[...], NT)
        first_out.ref[:, cols] = first.astype(bf16)
        to_message(first * twiddle()[a : a + 1, :], a, turned, stage)
    first_out.store()
    pack(stage, send.ref)


def transpose_up(ins, outs):
    (up,) = ins
    outs[0].ref[...] = up()[...].astype(f32).T.astype(bf16)


def prepare(ins, outs):
    outer, kernel = ins
    outer_t, kernel_t = outs
    outer_t.ref[...] = outer()[...].astype(f32).T.astype(bf16)
    parts = [kernel()[:, b, :].T for b in range(COLS)]
    kernel_t.ref[...] = jnp.concatenate(parts, axis=1).astype(bf16)


def columns(ins, outs):
    recv, outer, kernel, outer_t = ins
    send, spec_out = outs
    spec = dot(outer()[...], recv()[...])
    spec_out.ref[...] = spec.astype(bf16)
    spec_out.store()
    scaled = (kernel()[...].astype(f32) * spec).astype(bf16)
    send.ref[...] = dot(outer_t()[...], scaled).astype(bf16)


def columns_wide(ins, outs, stage):
    recv, outer, kernel, outer_t = ins
    send, spec_out = outs
    unpack_wide(recv(), stage)
    tiles = LANES // LANE_TILE
    rows = jnp.concatenate([stage[k].reshape(OUTER, LANE_TILE).astype(bf16) for k in range(tiles)], axis=1)
    spec = dot(outer()[...], rows)
    spec_out.ref[...] = spec
    spec_out.store()
    total = jnp.sum(recv()[:, :, MIXED:].astype(f32), axis=0, keepdims=True)
    send.ref[:, :, MIXED:] = jnp.broadcast_to(total, (NSEQ, 2, WIDE - MIXED)).astype(bf16)
    scaled = (kernel()[...].astype(f32) * spec).astype(bf16)
    back = dot(outer_t()[...], scaled)
    for k in range(tiles):
        stage[k] = back[:, lane_tile(k)].reshape(NSEQ, ROWS, LANE_TILE)
    pack_wide(stage, send.ref)


def mlp(ins, outs, turned, stage, turned_out, stage_out, down_own, grad_up, grad_down):
    recv, w, twiddle, x_in, up, shared, up_t, cot = ins
    send, later, direct = outs
    me = lax.axis_index("chan")
    unpack(recv(), stage)

    def forward(a):
        cols = token_columns(a)
        back = from_message(a, turned, stage)
        mixing = dot((back * twiddle()[a : a + 1, :]).astype(bf16), w()[...])
        x = x_in()[:, cols]
        low = (x + x * mixing).astype(bf16)
        hidden = dot(up()[...], low)
        cumulative = 0.5 * (1.0 + lax.erf(hidden * (1.0 / math.sqrt(2.0))))
        density = jnp.exp(-0.5 * hidden * hidden) * (1.0 / math.sqrt(2.0 * math.pi))
        act = (hidden * cumulative).astype(bf16)
        return back, mixing, low, act, cumulative + hidden * density

    def backward(a, back, mixing, low, act, slope):
        cols = token_columns(a)
        if a == 0:
            column = lax.broadcasted_iota(jnp.int32, (SLICE, HB), 1)
            own = column == lax.broadcasted_iota(jnp.int32, (SLICE, HB), 0) + me * SLICE
            own = jnp.where(own, 1.0, 0.0).astype(bf16)
            for p in range(NBLK):
                down_own[p * SLICE : (p + 1) * SLICE, :] = dot(own, shared()[p, :, TOK:], NT).astype(bf16)
        grad_act = []
        for p in range(NBLK):
            rows = slice(p * SLICE, (p + 1) * SLICE)
            grad_act.append(dot(down_own[rows, :], shared()[p, :, cols]).astype(bf16))
        grad_act = jnp.concatenate(grad_act, axis=0).astype(f32)
        down_part = [
            dot(act[2 * p * SLICE : 2 * (p + 1) * SLICE], shared()[2 * p : 2 * p + 2, :, cols].reshape(2 * BW, INNER), NT)
            for p in range(NBLK // 2)
        ]
        down_part = jnp.concatenate(down_part, axis=0)
        grad_hidden = (grad_act * slope).astype(bf16)
        up_part = dot(grad_hidden, low, NT)
        if a == 0:
            grad_up[...] = up_part
            grad_down[...] = down_part
        else:
            grad_up[...] += up_part
            grad_down[...] += down_part
        grad_gated = cot()[:, cols] + dot(up_t()[...], grad_hidden)
        direct.ref[:, cols] = grad_gated * (1.0 + mixing)
        direct.store(slice(None), cols)
        grad_mix = (grad_gated * x_in()[:, cols]).astype(bf16)
        second = dot(grad_mix, w()[...], NT)
        later.ref[a : a + 1, :] = jnp.sum(second * back, axis=0, keepdims=True)
        to_message(second * twiddle()[a : a + 1, :], a, turned_out, stage_out)

    held = [forward(0)]
    for a in range(ROWS):
        if a + 1 < ROWS:
            held.append(forward(a + 1))
        backward(a, *held.pop(0))
    pack_wide(stage_out, send.ref)
    grads = [grad_up[...]]
    for p in range(NBLK):
        grads.append(grad_down[p * SLICE : (p + 1) * SLICE, p % 2 * BW : (p % 2 + 1) * BW])
    grads = jnp.concatenate(grads, axis=0)
    pieces = [grads[i * 2 * NSEQ : (i + 1) * 2 * NSEQ] for i in range(PIECES)]
    pieces.append(jnp.zeros((2 * NSEQ, WIDE - MIXED - PIECES * BW), f32))
    grads = jnp.concatenate(pieces, axis=1).reshape(NSEQ, 2, WIDE - MIXED)
    send.ref[:, :, MIXED:] = grads.astype(bf16)


def gather_over_chan(block):
    steps = ((1, 0), (0, 1), (0, 3), (1, 2))
    straight = lax.optimization_barrier([lax.ppermute(block, "chan", step_to(step)) for step in steps])
    across, far = straight[0], straight[3]
    onward = [
        lax.ppermute(values, "chan", step_to(step)) for values, step in ((far, (1, 0)), (across, (0, 1)), (across, (0, 3)))
    ]
    return [block, *straight, *onward]


def block_places(ref):
    me = lax.axis_index("chan")
    steps = ((0, 0), (1, 0), (0, 3), (0, 1), (1, 2), (0, 2), (1, 3), (1, 1))
    return [ref.at[(me // 4 + dy) % 2 * 4 + (me % 4 + dx) % 4] for dy, dx in steps]


def twiddle_terms(ins, outs, turned, stage):
    recv, first, later = ins
    (shared,) = outs
    unpack_wide(recv(), stage)
    terms = []
    for a in range(ROWS):
        grad_back = from_message(a, turned, stage)
        early = jnp.sum(grad_back * first()[:, token_columns(a)].astype(f32), axis=0, keepdims=True)
        terms.append(early + later()[a : a + 1, :])
    terms = jnp.concatenate(terms, axis=0)
    terms = jnp.concatenate([terms[:, :LANE_TILE], terms[:, LANE_TILE:]], axis=0).astype(bf16)
    grads = weight_grads(recv())[HB:]
    zeros = jnp.zeros((SLICE, LANE_TILE - BW), f32)
    for p in range(NBLK):
        rows = slice(p * SLICE, (p + 1) * SLICE)
        shared.ref[p, :SLICE, :] = jnp.concatenate([grads[rows], zeros], axis=1).astype(bf16)
        shared.ref[p, SLICE:, :] = terms


def weight_grads(recv_ref):
    grads = recv_ref[:, :, MIXED:].astype(f32).reshape(2 * NSEQ, WIDE - MIXED)
    return jnp.concatenate([grads[:, i * BW : (i + 1) * BW] for i in range(PIECES)], axis=0)


def rows_out(ins, outs, turned, stage):
    recv, twiddle, w, direct = ins
    out, grad_up = outs
    unpack_wide(recv(), stage)
    for a in range(ROWS):
        cols = token_columns(a)
        grad_back = from_message(a, turned, stage)
        out.ref[:, cols] = direct()[:, cols] + dot((grad_back * twiddle()[a : a + 1, :]).astype(bf16), w()[...])
        out.store(slice(None), cols)
    grad_up.ref[...] = weight_grads(recv())[:HB] * (1.0 / math.sqrt(SEQ))


def finish(ins, outs):
    (shared,) = ins
    grad_down, grad_twiddle = outs
    terms = jnp.sum(shared()[:, SLICE:, :].astype(f32), axis=0) * (1.0 / math.sqrt(D))
    grad_twiddle.ref[:, :LANE_TILE] = terms[:ROWS]
    grad_twiddle.ref[:, LANE_TILE:] = terms[ROWS:]
    down = jnp.concatenate([shared()[j, :SLICE, :].astype(f32) for j in range(NBLK)], axis=0)
    grad_down.ref[...] = down.T[:BW] * (1.0 / math.sqrt(SEQ))


def exchange(values):
    return lax.all_to_all(
        values.reshape(NSEQ, -1, values.shape[-1]), "seq", split_axis=0, concat_axis=0, tiled=True
    ).reshape(values.shape)


def step_to(step):
    dy, dx = step
    return [(y * 4 + x, (y + dy) % 2 * 4 + (x + dx) % 4) for y in range(2) for x in range(4)]


def on_device(inputs, cotangent, kernel, inner_weight, outer_weight, twiddle, up_weight, down_weight):
    mix_flops = 2 * BW * TOK * INNER
    col_flops = 4 * OUTER * OUTER * LANES
    mlp_flops = 2 * HB * BW * TOK
    send, first = call(
        rows_in,
        [((OUTER, LANES), bf16), ((BW, TOK), bf16)],
        inputs,
        inner_weight,
        twiddle,
        flops=mix_flops,
        scratch=[TURNED, STAGE],
        arrived=(),
        grant=60,
    )

    cotangent_late, down_late, send = lax.optimization_barrier((cotangent, down_weight, send))
    block = jnp.concatenate([cotangent_late.astype(bf16), down_late], axis=1)
    shared = Stacked(gather_over_chan(block), (NBLK, BW, TOK + HB), block_places)

    kernel_late, send = lax.optimization_barrier((kernel, send))
    outer_t, kernel_t = call(
        prepare, [((OUTER, OUTER), bf16), ((OUTER, LANES), bf16)], outer_weight, kernel_late, arrived=()
    )
    (up_t,) = call(transpose_up, [((BW, HB), bf16)], up_weight, flops=HIDE_FLOPS, arrived=())

    recv = exchange(send)
    send, spectrum = call(
        columns,
        [((OUTER, LANES), bf16), ((OUTER, LANES), bf16)],
        recv,
        outer_weight,
        kernel_t,
        outer_t,
        flops=col_flops,
    )
    recv = exchange(send)
    send, later, direct = call(
        mlp,
        [((NSEQ, 2, WIDE), bf16), ((ROWS, INNER), f32), ((BW, TOK), f32)],
        recv,
        inner_weight,
        twiddle,
        inputs,
        up_weight,
        shared,
        up_t,
        cotangent,
        arrived=(0, 5),
        grant=60,
        flops=2 * mix_flops + 5 * mlp_flops,
        trans=2 * HB * TOK,
        scratch=[
            TURNED,
            STAGE,
            TURNED,
            STAGE,
            pltpu.VMEM((HB, BW), bf16),
            pltpu.VMEM((HB, BW), f32),
            pltpu.VMEM((HB, 2 * BW), f32),
        ],
    )
    recv = exchange(send)

    send, grad_spec = call(
        columns_wide,
        [((NSEQ, 2, WIDE), bf16), ((OUTER, LANES), f32)],
        recv,
        outer_weight,
        kernel_t,
        outer_t,
        flops=col_flops,
        scratch=[STAGE],
    )
    recv = exchange(send)
    grad_kernel = (grad_spec * spectrum.astype(f32)).reshape(OUTER, COLS, BW).transpose(2, 1, 0)

    (shared,) = call(
        twiddle_terms,
        [((NBLK, SLICE + 2 * ROWS, LANE_TILE), bf16)],
        recv,
        first,
        later,
        scratch=[TURNED, STAGE],
    )
    shared = lax.all_to_all(shared, "chan", split_axis=0, concat_axis=0, tiled=True)
    grad_inputs, grad_up = call(
        rows_out,
        [((BW, TOK), f32), ((HB, BW), f32)],
        recv,
        twiddle,
        inner_weight,
        direct,
        flops=mix_flops,
        scratch=[TURNED, STAGE],
    )
    grad_down, grad_twiddle = call(finish, [((BW, HB), f32), ((ROWS, INNER), f32)], shared)
    return grad_inputs, grad_kernel, grad_up, grad_down, grad_twiddle


def solution(mesh):
    placed = (
        P("chan", "seq"),
        P("chan", "seq"),
        P("chan", "seq", None),
        P(),
        P(),
        P("seq", None),
        P("chan", None),
        P("chan", None),
    )
    return jax.shard_map(
        on_device,
        mesh=mesh,
        in_specs=placed,
        out_specs=(
            P("chan", "seq"),
            P("chan", "seq", None),
            P("chan", None),
            P("chan", None),
            P("seq", None),
        ),
        check_vma=False,
    )
```

```python
import functools
import math

import jax
import jax.numpy as jnp
from jax import lax
from jax.experimental import pallas as pl
from jax.experimental.pallas import tpu as pltpu
from jax.sharding import PartitionSpec as P

D = 768
HID = 3072
NBLK = 8
OUTER = 512
INNER = 256
SEQ = 131072
BW = D // NBLK
HB = HID // NBLK
SLICE = HB // NBLK
NSEQ = 64
ROWS = OUTER // NSEQ
COLS = INNER // NSEQ
LANES = COLS * BW
TOK = ROWS * INNER
LANE_TILE = 128
MIXED = ROWS // 2 * LANES
PIECES = 2 * HB // (2 * NSEQ)
WIDE = MIXED + (PIECES * BW + LANE_TILE - 1) // LANE_TILE * LANE_TILE

f32 = jnp.float32
bf16 = jnp.bfloat16
HIDE_FLOPS = 14 * 10**9
NT = (((1,), (1,)), ((), ()))
NN = (((1,), (0,)), ((), ()))


def dot(lhs, rhs, dims=NN):
    return lax.dot_general(lhs, rhs, dims, preferred_element_type=f32)


class Stacked:
    def __init__(self, parts, shape, places):
        self.parts, self.shape, self.places = parts, shape, places
        self.dtype = parts[0].dtype


def call(body, outs, *operands, flops=0, scratch=(), trans=0, arrived=(0,), grant=32):
    shapes = [jax.ShapeDtypeStruct(shape, dtype) for shape, dtype in outs]
    nbytes = sum(math.prod(o.shape) * o.dtype.itemsize for o in list(operands) + shapes)
    arrays, specs = [], []
    for i, operand in enumerate(operands):
        parts = list(operand.parts) if isinstance(operand, Stacked) else [operand]
        arrays += parts
        specs += [pl.BlockSpec(memory_space=pl.ANY if i in arrived else pltpu.HBM)] * len(parts)
    n_in, n_out = len(operands), len(shapes)

    def kernel(*refs):
        sources, targets, refs = refs[: len(arrays)], refs[len(arrays) : len(arrays) + n_out], refs[len(arrays) + n_out :]
        held, built, refs = refs[:n_in], refs[n_in : n_in + n_out], refs[n_in + n_out :]
        in_sems, out_sems, refs = refs[0], refs[1], refs[2:]
        loads, taken = [], 0
        for operand, ref in zip(operands, held):
            if isinstance(operand, Stacked):
                places = operand.places(ref)
            else:
                places = [ref]
            copies = []
            for place in places:
                copies.append(pltpu.make_async_copy(sources[taken], place, in_sems.at[taken]))
                copies[-1].start()
                taken += 1
            loads.append(copies)

        def ready(i):
            while loads[i]:
                loads[i].pop().wait()
            return held[i]

        stores = []

        class Out:
            def __init__(self, i):
                self.i, self.ref, self.parts = i, built[i], 0

            def store(self, *index):
                source = built[self.i].at[index] if index else built[self.i]
                target = targets[self.i].at[index] if index else targets[self.i]
                copy = pltpu.make_async_copy(source, target, out_sems.at[self.i, self.parts])
                self.parts += 1
                copy.start()
                stores.append(copy)

        out = [Out(i) for i in range(n_out)]
        body([functools.partial(ready, i) for i in range(n_in)], out, *refs)
        for i in range(n_in):
            ready(i)
        for o in out:
            if not o.parts:
                o.store()
        for copy in stores:
            copy.wait()

    return pl.pallas_call(
        kernel,
        out_shape=shapes,
        in_specs=specs,
        out_specs=[pl.BlockSpec(memory_space=pltpu.HBM)] * n_out,
        scratch_shapes=[pltpu.VMEM(o.shape, o.dtype) for o in list(operands) + shapes]
        + [pltpu.SemaphoreType.DMA((len(arrays),)), pltpu.SemaphoreType.DMA((n_out, ROWS))]
        + list(scratch),
        cost_estimate=pl.CostEstimate(flops=flops, bytes_accessed=nbytes, transcendentals=trans),
        compiler_params=pltpu.CompilerParams(vmem_limit_bytes=grant * 1024 * 1024),
    )(*arrays)


def token_columns(a):
    return slice(a * INNER, (a + 1) * INNER)


def to_message(value, a, turned, stage):
    turned[:, :BW] = value.T
    parts = [turned[pl.ds(b, NSEQ, stride=COLS), :][:, :BW] for b in range(COLS)]
    row = jnp.concatenate(parts, axis=1)
    for k in range(LANES // LANE_TILE):
        stage[k, :, a, :] = row[:, k * LANE_TILE : (k + 1) * LANE_TILE]


def from_message(a, turned, stage):
    row = jnp.concatenate(
        [stage[k, :, a, :] for k in range(LANES // LANE_TILE)], axis=1
    )
    for b in range(COLS):
        turned[pl.ds(b, NSEQ, stride=COLS), :] = jnp.concatenate(
            [row[:, b * BW : (b + 1) * BW], jnp.zeros((NSEQ, LANE_TILE - BW), f32)], axis=1
        )
    return turned[...].T[:BW]


def lane_tile(k):
    return slice(k * LANE_TILE, (k + 1) * LANE_TILE)


def pack(stage, send_ref):
    for k in range(LANES // LANE_TILE):
        send_ref[:, lane_tile(k)] = stage[k].reshape(OUTER, LANE_TILE).astype(bf16)


def unpack(recv_ref, stage):
    for k in range(LANES // LANE_TILE):
        stage[k] = recv_ref[:, lane_tile(k)].astype(f32).reshape(NSEQ, ROWS, LANE_TILE)


def pairs():
    tiles = LANES // LANE_TILE
    return [(h * tiles + k, slice(2 * h, 2 * h + 2), k) for h in range(ROWS // 2) for k in range(tiles)]


def pack_wide(stage, send_ref):
    for tile, rows, k in pairs():
        send_ref[:, :, lane_tile(tile)] = stage[k, :, rows, :].astype(bf16)


def unpack_wide(recv_ref, stage):
    for tile, rows, k in pairs():
        stage[k, :, rows, :] = recv_ref[:, :, lane_tile(tile)].astype(f32)


STAGE = pltpu.VMEM((LANES // LANE_TILE, NSEQ, ROWS, LANE_TILE), f32)
TURNED = pltpu.VMEM((INNER, LANE_TILE), f32)


def rows_in(ins, outs, turned, stage):
    x, w, twiddle = ins
    send, first_out = outs
    for a in range(ROWS):
        cols = token_columns(a)
        first = dot(x()[:, cols].astype(bf16), w()[...], NT)
        first_out.ref[:, cols] = first.astype(bf16)
        to_message(first * twiddle()[a : a + 1, :], a, turned, stage)
    first_out.store()
    pack(stage, send.ref)


def transpose_up(ins, outs):
    (up,) = ins
    outs[0].ref[...] = up()[...].astype(f32).T.astype(bf16)


def prepare(ins, outs):
    outer, kernel = ins
    outer_t, kernel_t = outs
    outer_t.ref[...] = outer()[...].astype(f32).T.astype(bf16)
    parts = [kernel()[:, b, :].T for b in range(COLS)]
    kernel_t.ref[...] = jnp.concatenate(parts, axis=1).astype(bf16)


def columns(ins, outs):
    recv, outer, kernel, outer_t = ins
    send, spec_out = outs
    spec = dot(outer()[...], recv()[...])
    spec_out.ref[...] = spec.astype(bf16)
    spec_out.store()
    scaled = (kernel()[...].astype(f32) * spec).astype(bf16)
    send.ref[...] = dot(outer_t()[...], scaled).astype(bf16)


def columns_wide(ins, outs, stage):
    recv, outer, kernel, outer_t = ins
    send, spec_out = outs
    unpack_wide(recv(), stage)
    tiles = LANES // LANE_TILE
    rows = jnp.concatenate([stage[k].reshape(OUTER, LANE_TILE).astype(bf16) for k in range(tiles)], axis=1)
    spec = dot(outer()[...], rows)
    spec_out.ref[...] = spec
    spec_out.store()
    total = jnp.sum(recv()[:, :, MIXED:].astype(f32), axis=0, keepdims=True)
    send.ref[:, :, MIXED:] = jnp.broadcast_to(total, (NSEQ, 2, WIDE - MIXED)).astype(bf16)
    scaled = (kernel()[...].astype(f32) * spec).astype(bf16)
    back = dot(outer_t()[...], scaled)
    for k in range(tiles):
        stage[k] = back[:, lane_tile(k)].reshape(NSEQ, ROWS, LANE_TILE)
    pack_wide(stage, send.ref)


def mlp(ins, outs, turned, stage, turned_out, stage_out, down_own, grad_up, grad_down):
    recv, w, twiddle, x_in, up, shared, up_t, cot = ins
    send, later, direct = outs
    me = lax.axis_index("chan")
    unpack(recv(), stage)

    def forward(a):
        cols = token_columns(a)
        back = from_message(a, turned, stage)
        mixing = dot((back * twiddle()[a : a + 1, :]).astype(bf16), w()[...])
        x = x_in()[:, cols]
        low = (x + x * mixing).astype(bf16)
        hidden = dot(up()[...], low)
        cumulative = 0.5 * (1.0 + lax.erf(hidden * (1.0 / math.sqrt(2.0))))
        density = jnp.exp(-0.5 * hidden * hidden) * (1.0 / math.sqrt(2.0 * math.pi))
        act = (hidden * cumulative).astype(bf16)
        return back, mixing, low, act, cumulative + hidden * density

    def backward(a, back, mixing, low, act, slope):
        cols = token_columns(a)
        if a == 0:
            column = lax.broadcasted_iota(jnp.int32, (SLICE, HB), 1)
            own = column == lax.broadcasted_iota(jnp.int32, (SLICE, HB), 0) + me * SLICE
            own = jnp.where(own, 1.0, 0.0).astype(bf16)
            for p in range(NBLK):
                down_own[p * SLICE : (p + 1) * SLICE, :] = dot(own, shared()[p, :, TOK:], NT).astype(bf16)
        grad_act = []
        for p in range(NBLK):
            rows = slice(p * SLICE, (p + 1) * SLICE)
            grad_act.append(dot(down_own[rows, :], shared()[p, :, cols]).astype(bf16))
        grad_act = jnp.concatenate(grad_act, axis=0).astype(f32)
        down_part = [
            dot(act[2 * p * SLICE : 2 * (p + 1) * SLICE], shared()[2 * p : 2 * p + 2, :, cols].reshape(2 * BW, INNER), NT)
            for p in range(NBLK // 2)
        ]
        down_part = jnp.concatenate(down_part, axis=0)
        grad_hidden = (grad_act * slope).astype(bf16)
        up_part = dot(grad_hidden, low, NT)
        if a == 0:
            grad_up[...] = up_part
            grad_down[...] = down_part
        else:
            grad_up[...] += up_part
            grad_down[...] += down_part
        grad_gated = cot()[:, cols] + dot(up_t()[...], grad_hidden)
        direct.ref[:, cols] = grad_gated * (1.0 + mixing)
        direct.store(slice(None), cols)
        grad_mix = (grad_gated * x_in()[:, cols]).astype(bf16)
        second = dot(grad_mix, w()[...], NT)
        later.ref[a : a + 1, :] = jnp.sum(second * back, axis=0, keepdims=True)
        to_message(second * twiddle()[a : a + 1, :], a, turned_out, stage_out)

    held = [forward(0)]
    for a in range(ROWS):
        if a + 1 < ROWS:
            held.append(forward(a + 1))
        backward(a, *held.pop(0))
    pack_wide(stage_out, send.ref)
    grads = [grad_up[...]]
    for p in range(NBLK):
        grads.append(grad_down[p * SLICE : (p + 1) * SLICE, p % 2 * BW : (p % 2 + 1) * BW])
    grads = jnp.concatenate(grads, axis=0)
    pieces = [grads[i * 2 * NSEQ : (i + 1) * 2 * NSEQ] for i in range(PIECES)]
    pieces.append(jnp.zeros((2 * NSEQ, WIDE - MIXED - PIECES * BW), f32))
    grads = jnp.concatenate(pieces, axis=1).reshape(NSEQ, 2, WIDE - MIXED)
    send.ref[:, :, MIXED:] = grads.astype(bf16)


def gather_over_chan(block):
    steps = ((1, 0), (0, 1), (0, 3), (1, 2))
    straight = lax.optimization_barrier([lax.ppermute(block, "chan", step_to(step)) for step in steps])
    across, far = straight[0], straight[3]
    onward = [
        lax.ppermute(values, "chan", step_to(step)) for values, step in ((far, (1, 0)), (across, (0, 1)), (across, (0, 3)))
    ]
    return [block, *straight, *onward]


def block_places(ref):
    me = lax.axis_index("chan")
    steps = ((0, 0), (1, 0), (0, 3), (0, 1), (1, 2), (0, 2), (1, 3), (1, 1))
    return [ref.at[(me // 4 + dy) % 2 * 4 + (me % 4 + dx) % 4] for dy, dx in steps]


def twiddle_terms(ins, outs, turned, stage):
    recv, first, later = ins
    (shared,) = outs
    unpack_wide(recv(), stage)
    terms = []
    for a in range(ROWS):
        grad_back = from_message(a, turned, stage)
        early = jnp.sum(grad_back * first()[:, token_columns(a)].astype(f32), axis=0, keepdims=True)
        terms.append(early + later()[a : a + 1, :])
    terms = jnp.concatenate(terms, axis=0)
    terms = jnp.concatenate([terms[:, :LANE_TILE], terms[:, LANE_TILE:]], axis=0).astype(bf16)
    grads = weight_grads(recv())[HB:]
    zeros = jnp.zeros((SLICE, LANE_TILE - BW), f32)
    for p in range(NBLK):
        rows = slice(p * SLICE, (p + 1) * SLICE)
        shared.ref[p, :SLICE, :] = jnp.concatenate([grads[rows], zeros], axis=1).astype(bf16)
        shared.ref[p, SLICE:, :] = terms


def weight_grads(recv_ref):
    grads = recv_ref[:, :, MIXED:].astype(f32).reshape(2 * NSEQ, WIDE - MIXED)
    return jnp.concatenate([grads[:, i * BW : (i + 1) * BW] for i in range(PIECES)], axis=0)


def rows_out(ins, outs, turned, stage):
    recv, twiddle, w, direct = ins
    out, grad_up = outs
    unpack_wide(recv(), stage)
    for a in range(ROWS):
        cols = token_columns(a)
        grad_back = from_message(a, turned, stage)
        out.ref[:, cols] = direct()[:, cols] + dot((grad_back * twiddle()[a : a + 1, :]).astype(bf16), w()[...])
        out.store(slice(None), cols)
    grad_up.ref[...] = weight_grads(recv())[:HB] * (1.0 / math.sqrt(SEQ))


def finish(ins, outs):
    (shared,) = ins
    grad_down, grad_twiddle = outs
    terms = jnp.sum(shared()[:, SLICE:, :].astype(f32), axis=0) * (1.0 / math.sqrt(D))
    grad_twiddle.ref[:, :LANE_TILE] = terms[:ROWS]
    grad_twiddle.ref[:, LANE_TILE:] = terms[ROWS:]
    down = jnp.concatenate([shared()[j, :SLICE, :].astype(f32) for j in range(NBLK)], axis=0)
    grad_down.ref[...] = down.T[:BW] * (1.0 / math.sqrt(SEQ))


def exchange(values):
    return lax.all_to_all(
        values.reshape(NSEQ, -1, values.shape[-1]), "seq", split_axis=0, concat_axis=0, tiled=True
    ).reshape(values.shape)


def step_to(step):
    dy, dx = step
    return [(y * 4 + x, (y + dy) % 2 * 4 + (x + dx) % 4) for y in range(2) for x in range(4)]


def on_device(inputs, cotangent, kernel, inner_weight, outer_weight, twiddle, up_weight, down_weight):
    mix_flops = 2 * BW * TOK * INNER
    col_flops = 4 * OUTER * OUTER * LANES
    mlp_flops = 2 * HB * BW * TOK
    send, first = call(
        rows_in,
        [((OUTER, LANES), bf16), ((BW, TOK), bf16)],
        inputs,
        inner_weight,
        twiddle,
        flops=mix_flops,
        scratch=[TURNED, STAGE],
        arrived=(),
        grant=60,
    )

    cotangent_late, down_late, send = lax.optimization_barrier((cotangent, down_weight, send))
    block = jnp.concatenate([cotangent_late.astype(bf16), down_late], axis=1)
    shared = Stacked(gather_over_chan(block), (NBLK, BW, TOK + HB), block_places)

    kernel_late, send = lax.optimization_barrier((kernel, send))
    outer_t, kernel_t = call(
        prepare, [((OUTER, OUTER), bf16), ((OUTER, LANES), bf16)], outer_weight, kernel_late, arrived=()
    )
    (up_t,) = call(transpose_up, [((BW, HB), bf16)], up_weight, flops=HIDE_FLOPS, arrived=())

    recv = exchange(send)
    send, spectrum = call(
        columns,
        [((OUTER, LANES), bf16), ((OUTER, LANES), bf16)],
        recv,
        outer_weight,
        kernel_t,
        outer_t,
        flops=col_flops,
    )
    recv = exchange(send)
    send, later, direct = call(
        mlp,
        [((NSEQ, 2, WIDE), bf16), ((ROWS, INNER), f32), ((BW, TOK), f32)],
        recv,
        inner_weight,
        twiddle,
        inputs,
        up_weight,
        shared,
        up_t,
        cotangent,
        arrived=(0, 5),
        grant=52,
        flops=2 * mix_flops + 5 * mlp_flops,
        trans=2 * HB * TOK,
        scratch=[
            TURNED,
            STAGE,
            TURNED,
            STAGE,
            pltpu.VMEM((HB, BW), bf16),
            pltpu.VMEM((HB, BW), f32),
            pltpu.VMEM((HB, 2 * BW), f32),
        ],
    )
    recv = exchange(send)

    send, grad_spec = call(
        columns_wide,
        [((NSEQ, 2, WIDE), bf16), ((OUTER, LANES), f32)],
        recv,
        outer_weight,
        kernel_t,
        outer_t,
        flops=col_flops,
        scratch=[STAGE],
    )
    recv = exchange(send)
    grad_kernel = (grad_spec * spectrum.astype(f32)).reshape(OUTER, COLS, BW).transpose(2, 1, 0)

    (shared,) = call(
        twiddle_terms,
        [((NBLK, SLICE + 2 * ROWS, LANE_TILE), bf16)],
        recv,
        first,
        later,
        scratch=[TURNED, STAGE],
    )
    shared = lax.all_to_all(shared, "chan", split_axis=0, concat_axis=0, tiled=True)
    grad_inputs, grad_up = call(
        rows_out,
        [((BW, TOK), f32), ((HB, BW), f32)],
        recv,
        twiddle,
        inner_weight,
        direct,
        flops=mix_flops,
        scratch=[TURNED, STAGE],
    )
    grad_down, grad_twiddle = call(finish, [((BW, HB), f32), ((ROWS, INNER), f32)], shared)
    return grad_inputs, grad_kernel, grad_up, grad_down, grad_twiddle


def solution(mesh):
    placed = (
        P("chan", "seq"),
        P("chan", "seq"),
        P("chan", "seq", None),
        P(),
        P(),
        P("seq", None),
        P("chan", None),
        P("chan", None),
    )
    return jax.shard_map(
        on_device,
        mesh=mesh,
        in_specs=placed,
        out_specs=(
            P("chan", "seq"),
            P("chan", "seq", None),
            P("chan", None),
            P("chan", None),
            P("seq", None),
        ),
        check_vma=False,
    )
```
